32 devices in a mesh: fsdp: 2 (over x), context: 4 (over z), tensor: 4 (over y, core).
Axes of the slice: x: 2, y: 2, z: 4, core: 2. Of those that a mesh axis runs over, the one named last changes fastest.
Arguments:
- residual_in: bfloat16 [2, 1024, 1536], P('fsdp', 'context'), may hold values from -12 to 12
- token_mask: int32 [2, 1024], P('fsdp'), may hold values from 0 to 1, as said below
- parent_blocks: int32 [2, 8], P('fsdp'), may hold values from 0 to 6, as said below
- expert_routes: int32 [2, 1024, 8], P('fsdp', 'context'), may hold values from 0 to 15, all different within a row; in each aligned block of 256 rows (0 to 255, 256 to 511, ..., all dimensions but the last counted through in order) at most 160 rows name the same one
- attn_gain: bfloat16 [1536], P('fsdp'), may hold values from 0.099609375 to 1.8984375
- query_weight: bfloat16 [1536, 1536], P('fsdp', 'tensor'), may hold values from -0.15625 to 0.15625
- key_weight: bfloat16 [1536, 512], P('fsdp', 'tensor'), may hold values from -0.15625 to 0.15625
- value_weight: bfloat16 [1536, 512], P('fsdp', 'tensor'), may hold values from -0.15625 to 0.15625
- output_weight: bfloat16 [1536, 1536], P('tensor', 'fsdp'), may hold values from -3 to 3
- ffn_gain: bfloat16 [1536], P('fsdp'), may hold values from 0.099609375 to 1.8984375
- router_weight: bfloat16 [1536, 16], P('fsdp'), may hold values from -0.078125 to 0.078125
- expert_weights: bfloat16 [16, 3, 1536, 512], P('fsdp', None, None, 'tensor'), may hold values from -2 to 2
- out_cotangent: float32 [2, 1024, 1536], P('fsdp', 'context'), may hold values from -6 to 6
Outputs:
- block_out: bfloat16 [2, 1024, 1536], P('fsdp', 'context')
- input_grad: float32 [2, 1024, 1536], P('fsdp', 'context')
- attn_gain_grad: float32 [1536], P('fsdp')
- query_grad: float32 [1536, 1536], P('fsdp', 'tensor')
- key_grad: float32 [1536, 512], P('fsdp', 'tensor')
- value_grad: float32 [1536, 512], P('fsdp', 'tensor')
- output_grad: float32 [1536, 1536], P('tensor', 'fsdp')
- ffn_gain_grad: float32 [1536], P('fsdp')
- router_grad: float32 [1536, 16], P('fsdp')
- expert_grad: float32 [16, 3, 1536, 512], P('fsdp', None, None, 'tensor')
- rms_stats: float32 [4], replicated
The draws below stay inside these ranges and needn't reach their ends.
Inputs may be any that keep to these rules, and one draw needn't show every extreme that they name: `token_mask`: within each block of 128 positions the tokens with 1 come first and there is at least one; the first 4 blocks of every tree hold no padding. `parent_blocks`: block 0 gives 0, block b gives b - 1 for 0 < b < 4, every later block b gives a block from 3 to b - 1, and block 7 gives 6. `expert_routes`: each token names 8 different experts; among the 256 positions of one tree on one index of context no expert is named more than 160 times, a bound that some block reaches in some of these aligned blocks.
All inputs are finite; a program needn't handle non-finite values.
Results may differ from the reference program's by a relative error of at most 0.015.
The reference program's roundings to bfloat16 on the way count: a program that leaves them out, or rounds other values in their place, can miss the bound.
Values may be sent and summed in bfloat16 or wider, within the bound.
A program may use at most 256 MiB of HBM per device.

```python
import math
from functools import partial
import jax
import jax.numpy as jnp
import numpy as np
from jax import lax

D = 1536
HEADS = 24
KV_HEADS = 8
HEAD_DIM = 64
FF = 512
TOPK = 8
EXPERTS = 16
CAP = 160
SEG = 128
LOC = 256
NB = 8
TREE_LEN = 1024
TREES = 2
N_CONTEXT = 4


def draw_residual_in(key, part):
    key_base, key_rows = jax.random.split(key, 2)
    full_shape = (TREES, TREE_LEN, D)
    position = jnp.arange(TREE_LEN, dtype=jnp.float32) / TREE_LEN
    row_scale = jnp.exp(jax.random.uniform(key_rows, (TREES, TREE_LEN, 1), minval=math.log(0.25), maxval=math.log(0.75)))
    row_scale = row_scale * (1.0 + 2.0 * position)[None, :, None]
    entries = jax.random.normal(key_base, full_shape)
    return jnp.clip(entries * row_scale, -12.0, 12.0).astype(jnp.bfloat16)


def draw_expert_weights(key, part):
    full_shape = (EXPERTS, 3, D, FF)
    scales = jnp.array([D ** (-0.5), D ** (-0.5), 0.4], jnp.float32)[None, :, None, None]
    entries = jnp.clip(jax.random.normal(key, full_shape), -5.0, 5.0)
    return (entries * scales).astype(jnp.bfloat16)


def draw_parent_blocks(key, part):
    block_index = jnp.arange(NB, dtype=jnp.int32)
    trunk_end = NB // 2
    random_bits = jax.random.randint(key, (TREES, NB), 0, 1 << 20)
    spread = jnp.maximum(block_index - trunk_end + 1, 1)
    branch = trunk_end - 1 + random_bits % spread[None, :]
    chain_parent = jnp.maximum(block_index - 1, 0)
    parents = jnp.where(block_index[None, :] >= trunk_end, branch, chain_parent[None, :])
    parents = jnp.where(block_index[None, :] == NB - 1, NB - 2, parents)
    return parents.astype(jnp.int32)


def draw_token_mask(key, part):
    lengths = jax.random.randint(key, (TREES, NB), SEG // 4, SEG + 1)
    block_index = jnp.arange(NB, dtype=jnp.int32)
    lengths = jnp.where(block_index[None, :] < NB // 2, SEG, lengths)
    offsets = jnp.arange(TREE_LEN, dtype=jnp.int32) % SEG
    per_token = jnp.repeat(lengths, SEG, axis=1)
    return (offsets[None, :] < per_token).astype(jnp.int32)


def block_levels(stream_key, extent, cuts, low, top_value):
    def one(dim, parts):
        steps = jax.random.uniform(jax.random.fold_in(jax.random.fold_in(stream_key, 6), dim), (parts,), jnp.float32, low / len(cuts), top_value / len(cuts))
        return jnp.repeat(jnp.exp(steps), extent[dim] // parts).reshape((-1,) + (1,) * (len(extent) - dim - 1))

    level = one(*cuts[0])
    for cut in cuts[1:]:
        level = level * one(*cut)
    return level


def deal_out(stream_key, own, number, rows, number_of, top, reach, skew):
    order = jax.random.permutation(stream_key, number_of)
    packed, ordinary = load_shares(number_of, rows * top, reach, skew, True), load_shares(number_of, rows * top, reach, skew, False)
    places = jnp.arange(number_of)

    def named(sizes, offset_by):
        used = int((sizes > 0).sum())
        fixed = max(1, used // 4)
        shifted = fixed + (places - fixed + offset_by * (used - fixed)) % max(1, number_of - fixed)
        return jnp.zeros((number_of,), jnp.int32).at[order[jnp.where(places < fixed, places, shifted)]].set(jnp.asarray(sizes, jnp.int32))

    sizes = jnp.where(number % 4 == 0, named(packed, number // 4), named(ordinary, number - number // 4 - 1))
    mixed = jax.random.permutation(jax.random.fold_in(own, 3), number_of)
    giver, taker = mixed[0:number_of // 2 * 2:2], mixed[1:number_of // 2 * 2:2]
    margin = jnp.minimum(sizes[giver] - 1, reach - sizes[taker]) // 2
    margin = jnp.where((giver == order[0]) | (taker == order[0]) | (sizes[taker] == 0), 0, jnp.maximum(margin, 0))
    shifted = jax.random.randint(jax.random.fold_in(own, 4), (number_of // 2,), 0, 1 << 20) % (margin + 1)
    sizes = sizes.at[giver].add(-shifted).at[taker].add(shifted)
    members = jnp.searchsorted(jnp.cumsum(sizes), jnp.arange(rows * top), side="right").astype(jnp.int32)
    grid = members.reshape(top, rows).T
    grid = grid[jax.random.permutation(jax.random.fold_in(own, 1), rows)]
    offset_by = jax.random.randint(jax.random.fold_in(own, 2), (rows, 1), 0, top)
    return jnp.take_along_axis(grid, (jnp.arange(top)[None, :] + offset_by) % top, axis=1)


def load_shares(number_of, total, bound, lean, full):
    loads = [(1 << 20) // math.isqrt(grade ** lean) + 1 for grade in range(1, number_of + 1)]
    largest = bound if full else min(bound, max(-(-total // number_of), total * loads[0] // sum(loads)))
    least = 1 if total - largest >= number_of - 1 else 0
    counts, rest = [largest] + [least] * (number_of - 1), total - largest - least * (number_of - 1)
    while rest > 0:
        candidates = [i for i in range(1, number_of) if counts[i] < largest] or [i for i in range(1, number_of) if counts[i] < bound]
        whole, budget = sum([loads[i] for i in candidates]), rest
        for i in candidates:
            addition = min(bound - counts[i], max(1, budget * loads[i] // whole), rest)
            counts[i] = counts[i] + addition
            rest = rest - addition
    return np.array(counts)


def noise(key, dims, deviation, reach, cuts=(), kind=jnp.bfloat16):
    values = jax.random.normal(key, dims, jnp.float32) * deviation
    if len(cuts) > 0:
        values = block_levels(key, dims, cuts, -0.22, 0.18) * values
    return jnp.clip(values, min=-reach, max=reach).astype(kind)


def setup_inputs(seed: int = 0) -> dict:
    keys = jax.random.split(jax.random.key(seed), 14)
    residual_in = draw_residual_in(jax.random.fold_in(keys[13], 71), 0)
    token_mask = draw_token_mask(jax.random.fold_in(keys[13], 71), 0)
    parent_blocks = draw_parent_blocks(jax.random.fold_in(keys[13], 71), 0)
    expert_routes_keys = jax.random.split(jax.random.fold_in(keys[3], 1), TREES * TREE_LEN // LOC)
    expert_routes_turns = jax.random.permutation(jax.random.fold_in(keys[3], 3), TREES * TREE_LEN // LOC)
    expert_routes = jax.vmap(lambda own, number: deal_out(jax.random.fold_in(keys[3], 2), own, number, LOC, EXPERTS, TOPK, CAP, 1))(expert_routes_keys, expert_routes_turns).reshape((TREES, TREE_LEN, TOPK))
    attn_gain = jnp.clip(1.0 + 0.18 * jax.random.normal(keys[4], (D,), jnp.float32), 0.099609375, 1.8984375).astype(jnp.bfloat16)
    query_weight = noise(keys[5], (D, HEADS * HEAD_DIM), D ** -0.5, 0.15625, ((0, 2), (1, 4)))
    key_weight = noise(keys[6], (D, KV_HEADS * HEAD_DIM), D ** -0.5, 0.15625, ((0, 2), (1, 4)))
    value_weight = noise(keys[7], (D, KV_HEADS * HEAD_DIM), D ** -0.5, 0.15625, ((0, 2), (1, 4)))
    output_weight = noise(keys[8], (HEADS * HEAD_DIM, D), 4 ** -0.5, 3.0, ((0, 4), (1, 2)))
    ffn_gain = jnp.clip(1.0 + 0.18 * jax.random.normal(keys[9], (D,), jnp.float32), 0.099609375, 1.8984375).astype(jnp.bfloat16)
    router_weight = noise(keys[10], (D, EXPERTS), (4 * D) ** -0.5, 0.078125, ((0, 2),))
    expert_weights = draw_expert_weights(jax.random.fold_in(keys[13], 71), 0)
    out_cotangent = noise(keys[12], (TREES, TREE_LEN, D), 1.0, 6.0, ((0, 2), (1, 4)), jnp.float32)
    return dict(residual_in=residual_in, token_mask=token_mask, parent_blocks=parent_blocks, expert_routes=expert_routes, attn_gain=attn_gain, query_weight=query_weight, key_weight=key_weight, value_weight=value_weight, output_weight=output_weight, ffn_gain=ffn_gain, router_weight=router_weight, expert_weights=expert_weights, out_cotangent=out_cotangent)


@jax.custom_vjp
def low(v):
    return lax.optimization_barrier(v.astype(jnp.bfloat16)).astype(jnp.float32)

@jax.custom_vjp
def low_back(v):
    return v

def low_keep(v):
    return (low(v), None)

def low_pass(kept, grad):
    return (grad,)

def back_keep(v):
    return (v, None)

def back_low(kept, grad):
    return (low(grad),)
low.defvjp(low_keep, low_pass)
low_back.defvjp(back_keep, back_low)
EPS = 1e-06
HIGH = lax.Precision.HIGHEST

def ancestry(parents):
    blocks = parents.shape[-1]
    block_range = jnp.arange(blocks, dtype=jnp.int32)
    current = block_range
    closure = jnp.zeros((blocks, blocks), jnp.int32)
    for walk_step in range(blocks):
        closure = jnp.maximum(closure, (current[:, None] == block_range[None, :]).astype(jnp.int32))
        current = parents[current].astype(jnp.int32)
    return closure

def rotary(values, angles):
    half_dim = values.shape[-1] // 2
    rotated = jnp.concatenate([-values[..., half_dim:], values[..., :half_dim]], -1)
    return values * jnp.cos(angles) + rotated * jnp.sin(angles)

def rms_normalize(values, gains):
    return values * lax.rsqrt(lax.optimization_barrier(jnp.mean(values * values, -1, keepdims=True)) + EPS) * gains

def tree_forward(params, stream, allowed, angles, routes, slot_index, token_of_slot):
    gain_one, w_query, w_key, w_value, w_output, gain_two, w_router, w_experts = params
    tree_len = stream.shape[0]
    group_size = HEADS // KV_HEADS
    normed_one = low(rms_normalize(stream, gain_one))
    queries = jnp.dot(normed_one, w_query, precision=HIGH).reshape(tree_len, HEADS, HEAD_DIM)
    keys_raw = jnp.dot(normed_one, w_key, precision=HIGH).reshape(tree_len, KV_HEADS, HEAD_DIM)
    values_raw = jnp.dot(normed_one, w_value, precision=HIGH).reshape(tree_len, KV_HEADS, HEAD_DIM)
    head_angles = angles[:, None, :]
    query_rot = low(rotary(low_back(queries), head_angles))
    key_rot = low(rotary(low_back(keys_raw), head_angles))
    value_low = low(low_back(values_raw))
    grouped = query_rot.reshape(tree_len, KV_HEADS, group_size, HEAD_DIM).transpose(1, 0, 2, 3)

    def one_head(operands):
        head_queries, head_keys, head_values = operands
        scores = low_back(jnp.einsum('lgh,mh->glm', head_queries, head_keys, precision=HIGH) * 0.125)
        scores = jnp.where(allowed[None] > 0, scores, -jnp.inf)
        weights = low(jax.nn.softmax(scores, -1))
        return jnp.einsum('glm,mh->lgh', weights, head_values, precision=HIGH)
    attended = lax.map(jax.checkpoint(one_head), (grouped, key_rot.transpose(1, 0, 2), value_low.transpose(1, 0, 2)))
    attended = attended.transpose(1, 0, 2, 3).reshape(tree_len, HEADS * HEAD_DIM)
    attended = low(low_back(attended))
    attn_out = low_back(jnp.dot(attended, w_output, precision=HIGH))
    middle = stream + attn_out
    normed_two = low(rms_normalize(middle, gain_two))
    logits = low_back(jnp.dot(normed_two, w_router, precision=HIGH))
    router_probs = jax.nn.softmax(logits, -1)
    gate_probs = jnp.take_along_axis(router_probs, routes, -1)
    padded = jnp.concatenate([normed_two, jnp.zeros((1, normed_two.shape[1]), normed_two.dtype)], 0)
    slot_rows = padded[token_of_slot]
    gate_up = jnp.einsum('erd,esdf->esrf', slot_rows, w_experts[:, :2], precision=HIGH)
    hidden = low(jax.nn.silu(low_back(gate_up[:, 0])) * low_back(gate_up[:, 1]))
    produced = low_back(jnp.einsum('erf,edf->erd', hidden, w_experts[:, 2], precision=HIGH))
    picked = produced.reshape(-1, produced.shape[-1])[slot_index].reshape(tree_len, TOPK, -1)
    ffn_out = lax.optimization_barrier(jnp.sum(gate_probs[..., None] * picked, 1))
    return (middle + ffn_out, (attn_out, middle, ffn_out))

def reference(residual_in, token_mask, parent_blocks, expert_routes, attn_gain, query_weight, key_weight, value_weight, output_weight, ffn_gain, router_weight, expert_weights, out_cotangent):
    params = (attn_gain.astype(jnp.float32), query_weight.astype(jnp.float32), key_weight.astype(jnp.float32), value_weight.astype(jnp.float32), output_weight.astype(jnp.float32), ffn_gain.astype(jnp.float32), router_weight.astype(jnp.float32), expert_weights.astype(jnp.float32))
    tree_len = residual_in.shape[1]
    model_width = residual_in.shape[2]
    tree_cap = CAP * N_CONTEXT
    positions = jnp.arange(tree_len, dtype=jnp.int32)
    block_ids = positions // SEG
    half_freq = 10000.0 ** (-(jnp.arange(HEAD_DIM // 2, dtype=jnp.float32) * 2.0) / HEAD_DIM)
    frequencies = jnp.concatenate([half_freq, half_freq])

    def one_tree(running, operands):
        grad_sums, square_sums, valid_sum = running
        stream_low, mask_row, parents, routes, cotangent = operands
        closure = ancestry(parents)
        block_depth = lax.optimization_barrier(jnp.sum(closure, -1)) - 1
        rope_pos = (block_depth[block_ids] * SEG + positions % SEG).astype(jnp.float32)
        angles = rope_pos[:, None] * frequencies[None, :]
        allowed = ((closure[block_ids][:, block_ids] > 0) & (positions[None, :] <= positions[:, None]) & (mask_row[None, :] > 0)).astype(jnp.int32)
        flat_routes = routes.reshape(-1)
        hot_int = (flat_routes[:, None] == jnp.arange(EXPERTS, dtype=jnp.int32)[None, :]).astype(jnp.int32)
        slot_rank = lax.optimization_barrier(jnp.sum((jnp.cumsum(hot_int, 0) - 1) * hot_int, -1))
        slot_index = flat_routes * tree_cap + slot_rank
        token_of_slot = jnp.full((EXPERTS * tree_cap,), tree_len, jnp.int32).at[slot_index].set(jnp.arange(tree_len * TOPK, dtype=jnp.int32) // TOPK).reshape(EXPERTS, tree_cap)
        stream = stream_low.astype(jnp.float32)
        forward = partial(tree_forward, allowed=allowed, angles=angles, routes=routes, slot_index=slot_index, token_of_slot=token_of_slot)
        block_out, pullback, extras = jax.vjp(forward, params, stream, has_aux=True)
        param_grads, stream_grad = pullback(cotangent.astype(jnp.float32))
        grad_sums = jax.tree.map(jnp.add, grad_sums, param_grads)
        mask_float = mask_row.astype(jnp.float32)
        terms = jnp.stack([jnp.sum(lax.optimization_barrier(jnp.sum(component * component, -1)) * mask_float) for component in (stream,) + extras])
        return ((grad_sums, square_sums + terms, valid_sum + jnp.sum(mask_float)), (block_out.astype(jnp.bfloat16), stream_grad))
    initial = (jax.tree.map(jnp.zeros_like, params), jnp.zeros((4,), jnp.float32), jnp.zeros((), jnp.float32))
    (grad_sums, square_sums, valid_sum), (block_out, input_grad) = lax.scan(one_tree, initial, (residual_in, token_mask, parent_blocks, expert_routes, out_cotangent))
    rms_stats = jnp.sqrt(square_sums / (valid_sum * model_width))
    return (block_out, input_grad, grad_sums[0], grad_sums[1], grad_sums[2], grad_sums[3], grad_sums[4], grad_sums[5], grad_sums[6], grad_sums[7], rms_stats)
```

```python
import jax
import jax.numpy as jnp
from jax import lax
from jax.sharding import PartitionSpec as P

HEAD_DIM = 64
SEG = 128
EPS = 1e-06
BF = jnp.bfloat16
F32 = jnp.float32


def ancestry(parents):
    blocks = parents.shape[-1]
    diagonal = jnp.eye(blocks, dtype=jnp.int32)
    upward = (parents[..., :, None] == jnp.arange(blocks, dtype=jnp.int32)).astype(jnp.int32)
    closure = jnp.minimum(diagonal + upward, 1)
    for squaring in range(blocks.bit_length()):
        closure = jnp.minimum(jnp.matmul(closure, closure), 1)
    return closure


def dot(spec, a, b):
    return jnp.einsum(spec, a, b, preferred_element_type=F32)


def swap_halves(u):
    half = u.shape[-1] // 2
    return jnp.concatenate([-u[..., half:], u[..., :half]], -1)


def norm_scale(z):
    return lax.rsqrt(jnp.mean(z * z, -1, keepdims=True) + EPS)


def norm_back(z, scale, gain, grad):
    u = grad * gain
    out = scale * u - z * (scale**3) * jnp.mean(u * z, -1, keepdims=True)
    return out, jnp.sum(grad * z * scale, 0)


def per_device(
    residual_in,
    token_mask,
    parent_blocks,
    expert_routes,
    attn_gain,
    query_weight,
    key_weight,
    value_weight,
    output_weight,
    ffn_gain,
    router_weight,
    expert_weights,
    out_cotangent,
):
    _, rows, width = residual_in.shape
    tree_len = token_mask.shape[1]
    blocks = parent_blocks.shape[1]
    experts_here = expert_weights.shape[0]
    ctx = lax.axis_index("context")
    fs = lax.axis_index("fsdp")
    n_fs = lax.axis_size("fsdp")
    n_ctx = lax.axis_size("context")
    experts = experts_here * n_fs

    stream = residual_in[0].astype(F32)
    cot = out_cotangent[0]
    cot_all = lax.all_gather(cot.astype(BF), ("fsdp", "context"), axis=0, tiled=True)
    gain_one = lax.all_gather(attn_gain, "fsdp", axis=0, tiled=True).astype(F32)
    gain_two = lax.all_gather(ffn_gain, "fsdp", axis=0, tiled=True).astype(F32)
    w_qkv = jnp.concatenate([query_weight, key_weight, value_weight], 1)
    w_qkv = lax.all_gather(w_qkv, "fsdp", axis=0, tiled=True)
    w_out = lax.all_gather(output_weight, "fsdp", axis=1, tiled=True)
    w_router = lax.all_gather(router_weight, "fsdp", axis=0, tiled=True)

    heads = query_weight.shape[1] // HEAD_DIM
    kv = key_weight.shape[1] // HEAD_DIM
    group = heads // kv
    q_cols, kv_cols = heads * HEAD_DIM, kv * HEAD_DIM

    positions = ctx * rows + jnp.arange(rows, dtype=jnp.int32)
    pick = (positions[:, None] // SEG == jnp.arange(blocks, dtype=jnp.int32)[None, :]).astype(jnp.int32)
    closure = ancestry(parent_blocks[0])
    row_reach = jnp.matmul(pick, closure)
    depth = jnp.matmul(pick, jnp.sum(closure, -1) - 1)
    rope_pos = (depth * SEG + positions % SEG).astype(F32)
    half_freq = 10000.0 ** (-(jnp.arange(HEAD_DIM // 2, dtype=F32) * 2.0) / HEAD_DIM)
    angles = rope_pos[:, None, None] * jnp.concatenate([half_freq, half_freq])
    cos, sin = jnp.cos(angles), jnp.sin(angles)
    key_pos = jnp.arange(tree_len, dtype=jnp.int32)
    allowed = (
        (jnp.repeat(row_reach, SEG, axis=1) > 0)
        & (key_pos[None, :] <= positions[:, None])
        & (token_mask[0][None, :] > 0)
    )

    scale_one = norm_scale(stream)
    normed_one = (stream * scale_one * gain_one).astype(BF)
    qkv = dot("ld,dc->lc", normed_one, w_qkv)

    def rot(u):
        u = u.reshape(rows, -1, HEAD_DIM)
        return (u * cos + swap_halves(u) * sin).astype(BF).reshape(rows, -1)

    def unrot(u):
        u = u.reshape(rows, -1, HEAD_DIM)
        return (u * cos - swap_halves(u) * sin).astype(BF).reshape(rows, -1)

    q = rot(qkv[:, :q_cols]).reshape(rows, kv, group, HEAD_DIM)
    k_own = rot(qkv[:, q_cols : q_cols + kv_cols])
    v_own = qkv[:, q_cols + kv_cols :].astype(BF)
    kv_all = lax.all_gather(jnp.concatenate([k_own, v_own], 1), "context", axis=0, tiled=True)
    k_all = kv_all[:, :kv_cols].reshape(tree_len, kv, HEAD_DIM)
    v_all = kv_all[:, kv_cols:].reshape(tree_len, kv, HEAD_DIM)

    scores = dot("lkgh,mkh->kglm", q, k_all) * 0.125
    masked = jnp.where(allowed, scores, -jnp.inf)
    peak = jnp.max(masked, -1, keepdims=True)
    log_total = peak + jnp.log(jnp.sum(jnp.exp(masked - peak), -1, keepdims=True))
    probs = jnp.exp(masked - log_total)
    probs_low = probs.astype(BF)
    attended = dot("kglm,mkh->lkgh", probs_low, v_all).astype(BF).reshape(rows, q_cols)
    attn_out = lax.psum(dot("lc,cd->ld", attended, w_out).astype(BF), "tensor").astype(F32)
    middle = stream + attn_out
    scale_two = norm_scale(middle)
    normed_two = (middle * scale_two * gain_two).astype(BF)

    logits = dot("ld,de->le", normed_two, w_router)
    router_probs = jax.nn.softmax(logits, -1)
    routes = expert_routes[0]
    used = jnp.any(routes[:, :, None] == jnp.arange(experts, dtype=jnp.int32), 1)
    gates = jnp.where(used, router_probs, 0.0)

    normed_all = lax.all_gather(normed_two, ("fsdp", "context"), axis=0, tiled=True)
    gates_all = lax.all_gather(gates, ("fsdp", "context"), axis=0, tiled=True)
    gates_here = lax.dynamic_slice_in_dim(gates_all, fs * experts_here, experts_here, 1)
    g3 = gates_here[:, :, None]
    gate_val = dot("td,edf->tef", normed_all, expert_weights[:, 0])
    up_val = dot("td,edf->tef", normed_all, expert_weights[:, 1])
    back = dot("td,edf->tef", cot_all, expert_weights[:, 2])
    sig = 1.0 / (1.0 + jnp.exp(-gate_val))
    act = gate_val * sig
    hid = act * up_val
    gated_hid = (g3 * hid).astype(BF)
    gate_grad_part = jnp.sum(hid * back, -1)
    d_hid = g3 * back
    d_gate_val = (d_hid * up_val * (sig * (1.0 + gate_val * (1.0 - sig)))).astype(BF)
    d_up_val = (d_hid * act).astype(BF)

    def own(z):
        z = z.reshape((n_fs, n_ctx, rows) + z.shape[1:])
        return lax.dynamic_index_in_dim(z, ctx, 1, keepdims=False)

    ffn_part = dot("stef,edf->std", own(gated_hid), expert_weights[:, 2])
    dn_part = dot("stef,edf->std", own(d_gate_val), expert_weights[:, 0]) + dot(
        "stef,edf->std", own(d_up_val), expert_weights[:, 1]
    )
    gate_part = lax.dynamic_update_slice_in_dim(
        jnp.zeros((n_fs, rows, experts), F32), own(gate_grad_part), fs * experts_here, 2
    )

    def home(z):
        z = lax.psum_scatter(z.astype(BF), "fsdp", scatter_dimension=0, tiled=True)
        return lax.psum(z, "tensor").astype(F32)[0]

    dn = home(dn_part)
    gate_grad = lax.psum(lax.psum_scatter(gate_part, "fsdp", scatter_dimension=0, tiled=True), "tensor")[0]
    ffn_out = home(ffn_part)
    block_out = middle + ffn_out

    expert_grad = jnp.stack(
        [
            dot("td,tef->edf", normed_all, d_gate_val),
            dot("td,tef->edf", normed_all, d_up_val),
            dot("td,tef->edf", cot_all, gated_hid),
        ],
        1,
    )

    own_mask = lax.dynamic_slice_in_dim(token_mask[0], ctx * rows, rows, 0).astype(F32)
    sums = [jnp.sum(jnp.sum(z * z, -1) * own_mask) for z in (stream, attn_out, middle, ffn_out)]
    sums = lax.psum(jnp.stack(sums + [jnp.sum(own_mask)]), ("fsdp", "context"))
    rms_stats = jnp.sqrt(sums[:4] / (sums[4] * width))

    prob_grad = jnp.where(used, gate_grad, 0.0)
    logit_grad = (router_probs * (prob_grad - jnp.sum(router_probs * prob_grad, -1, keepdims=True))).astype(BF)
    dn = dn + dot("le,de->ld", logit_grad, w_router)
    router_full = dot("ld,le->de", normed_two, logit_grad)
    mid_grad, ffn_gain_full = norm_back(middle, scale_two, gain_two, dn)
    middle_grad = cot + mid_grad
    d_attn = middle_grad.astype(BF)
    out_full = dot("lc,ld->cd", attended, d_attn)
    d_att = dot("ld,cd->lc", d_attn, w_out).astype(BF).reshape(rows, kv, group, HEAD_DIM)
    d_probs = dot("lkgh,mkh->kglm", d_att, v_all)
    delta = jnp.sum(probs * d_probs, -1, keepdims=True)
    d_scores = (probs * (d_probs - delta)).astype(BF)
    dq = dot("kglm,mkh->lkgh", d_scores, k_all) * 0.125
    dk = dot("kglm,lkgh->mkh", d_scores, q) * 0.125
    dv = dot("kglm,lkgh->mkh", probs_low, d_att)
    dkv = jnp.concatenate([dk.reshape(tree_len, kv_cols), dv.reshape(tree_len, kv_cols)], 1)
    dkv = lax.psum_scatter(dkv.astype(BF), "context", scatter_dimension=0, tiled=True).astype(F32)
    d_qkv = jnp.concatenate(
        [unrot(dq.reshape(rows, q_cols)), unrot(dkv[:, :kv_cols]), dkv[:, kv_cols:].astype(BF)], 1
    )
    qkv_full = dot("ld,lc->dc", normed_one, d_qkv)
    dn_one = lax.psum(dot("lc,dc->ld", d_qkv, w_qkv).astype(BF), "tensor").astype(F32)
    str_grad, attn_gain_full = norm_back(stream, scale_one, gain_one, dn_one)
    input_grad = middle_grad + str_grad

    qkv_part = lax.psum(lax.psum_scatter(qkv_full.astype(BF), "fsdp", scatter_dimension=0, tiled=True), "context").astype(F32)
    out_part = lax.psum(lax.psum_scatter(out_full.astype(BF), "fsdp", scatter_dimension=1, tiled=True), "context").astype(F32)
    small = jnp.concatenate([router_full, attn_gain_full[:, None], ffn_gain_full[:, None]], 1)
    small = lax.psum(lax.psum_scatter(small, "fsdp", scatter_dimension=0, tiled=True), "context")
    return (
        block_out.astype(BF)[None],
        input_grad[None],
        small[:, experts],
        qkv_part[:, :q_cols],
        qkv_part[:, q_cols : q_cols + kv_cols],
        qkv_part[:, q_cols + kv_cols :],
        out_part,
        small[:, experts + 1],
        small[:, :experts],
        expert_grad,
        rms_stats,
    )


def solution(mesh):
    return jax.shard_map(
        per_device,
        mesh=mesh,
        in_specs=(
            P("fsdp", "context", None),
            P("fsdp", None),
            P("fsdp", None),
            P("fsdp", "context", None),
            P("fsdp"),
            P("fsdp", "tensor"),
            P("fsdp", "tensor"),
            P("fsdp", "tensor"),
            P("tensor", "fsdp"),
            P("fsdp"),
            P("fsdp", None),
            P("fsdp", None, None, "tensor"),
            P("fsdp", "context", None),
        ),
        out_specs=(
            P("fsdp", "context", None),
            P("fsdp", "context", None),
            P("fsdp"),
            P("fsdp", "tensor"),
            P("fsdp", "tensor"),
            P("fsdp", "tensor"),
            P("tensor", "fsdp"),
            P("fsdp"),
            P("fsdp", None),
            P("fsdp", None, None, "tensor"),
            P(),
        ),
        check_vma=False,
    )
```

```python
import functools

import jax
import jax.numpy as jnp
from jax import lax
from jax.experimental import pallas as pl
from jax.experimental.pallas import tpu as pltpu
from jax.sharding import PartitionSpec as P

HEAD_DIM = 64
SEG = 128
EPS = 1e-06
BF = jnp.bfloat16
F32 = jnp.float32


MESH = pl.DeviceIdType.MESH
VM = pltpu.VMEM


def tdot(a, b, dims):
    return lax.dot_general(a, b, (dims, ((), ())), preferred_element_type=F32)


NN = ((1,), (0,))
NT = ((1,), (1,))
TN = ((0,), (0,))


def place():
    f, c, t = lax.axis_index("fsdp"), lax.axis_index("context"), lax.axis_index("tensor")
    core = lax.rem(t, 2)
    peers = dict(
        x=(1 - f, c, t), core=(f, c, t + 1 - 2 * core), y=(f, c, lax.rem(t + 2, 4))
    )
    return f, c, t, core, peers


def greet(c, n_ctx, peers, f, t):
    bar = pltpu.get_barrier_semaphore()
    for p in peers.values():
        pl.semaphore_signal(bar, inc=1, device_id=p, device_id_type=MESH)

    @pl.when(c > 0)
    def _():
        pl.semaphore_signal(bar, inc=1, device_id=(f, c - 1, t), device_id_type=MESH)

    @pl.when(c < n_ctx - 1)
    def _():
        pl.semaphore_signal(bar, inc=1, device_id=(f, c + 1, t), device_id_type=MESH)

    near = jnp.where(c > 0, 1, 0) + jnp.where(c < n_ctx - 1, 1, 0)
    pl.semaphore_wait(bar, len(peers) + near)


def remote(src, dst, send, recv, device):
    return pltpu.make_async_remote_copy(
        src_ref=src, dst_ref=dst, send_sem=send, recv_sem=recv, device_id=device, device_id_type=MESH
    )


class Gather:
    def __init__(self, buf, sems, n_ctx, where):
        self.buf, self.n = buf, n_ctx
        self.f, self.c, self.t, self.core, self.peers = where
        self.half = buf.shape[2] // 2
        self.zs, self.zr, self.xs, self.xr, self.ks, self.kr = sems

    @staticmethod
    def sems(n_ctx):
        d = pltpu.SemaphoreType.DMA
        return [d((2, n_ctx)), d((n_ctx,)), d((n_ctx,)), d((n_ctx,)), d((2, n_ctx)), d((2, n_ctx))]

    def part(self, f, c, core):
        return self.buf.at[f * self.n + c, :, pl.ds(pl.multiple_of(core * self.half, 128), self.half)]

    def z(self, side, block):
        r = self.part(self.f, block, self.core)
        return remote(r, r, self.zs.at[(side + 1) // 2, block], self.zr.at[block], (self.f, self.c + side, self.t))

    def x(self, block):
        r = self.part(self.f, block, self.core)
        return remote(r, r, self.xs.at[block], self.xr.at[block], self.peers["x"])

    def k(self, f, block):
        r = self.part(f, block, self.core)
        return remote(r, r, self.ks.at[f, block], self.kr.at[f, block], self.peers["core"])

    def there(self, c):
        return (c >= 0) & (c < self.n)

    def begin(self):
        c = self.c
        self.x(c).start()
        for side in (-1, 1):
            pl.when(self.there(c + side))(lambda side=side: self.z(side, c).start())

    def relay(self, d):
        for side in (-1, 1):
            block = self.c + side * d

            @pl.when(self.there(block))
            def _(side=side, block=block):
                self.z(-side, block).wait_recv()
                pl.when(self.there(self.c - side))(lambda: self.z(-side, block).start())
                self.x(block).start()
                self.k(self.f, block).start()

    def cross(self, block):
        r = self.part(1 - self.f, block, self.core)
        remote(r, r, self.xs.at[block], self.xr.at[block], self.peers["x"]).wait_recv()
        self.k(1 - self.f, block).start()

    def ready(self, f, block):
        r = self.part(f, block, 1 - self.core)
        remote(r, r, self.ks.at[f, block], self.kr.at[f, block], self.peers["core"]).wait_recv()

    def finish(self):
        c = self.c
        for b in range(self.n):
            self.x(b).wait_send()
            self.k(1 - self.f, b).wait_send()
            pl.when(c != b)(lambda b=b: self.k(self.f, b).wait_send())
            pl.when((b >= c) & (c > 0))(lambda b=b: self.z(-1, b).wait_send())
            pl.when((b <= c) & (c < self.n - 1))(lambda b=b: self.z(1, b).wait_send())


class Home:
    def __init__(self, refs, sems, where, width):
        self.part, self.r1, self.mine, self.b2, self.r2, self.b3, self.r3, self.total = refs
        self.send, self.recv = sems
        self.f, self.c, self.t, self.core, self.peers = where
        self.width = width

    @staticmethod
    def scratch(rows, width):
        w = width // 2 + 128
        return [
            VM((2, 2, rows, w), BF),
            VM((2, rows, w), BF),
            VM((rows, w), F32),
            VM((rows, w), BF),
            VM((rows, w), BF),
            VM((rows, w), BF),
            VM((rows, w), BF),
            VM((2, rows, width // 2), F32),
        ]

    def copy(self, i, src, dst, to):
        return remote(src, dst, self.send.at[i], self.recv.at[i], self.peers[to])

    def c1(self):
        return self.copy(0, self.part.at[1 - self.core], self.r1, "core")

    def c2(self):
        return self.copy(1, self.b2, self.r2, "x")

    def c3(self):
        return self.copy(2, self.b3, self.r3, "y")

    def c4(self):
        r = self.total.at[self.core]
        return self.copy(3, r, r, "core")

    def s1(self):
        self.c1().start()

    def s2(self):
        self.c1().wait_recv()
        f, core = self.f, self.core
        self.b2[...] = (self.part[core, 1 - f].astype(F32) + self.r1[1 - f].astype(F32)).astype(BF)
        self.c2().start()
        self.mine[...] = self.part[core, f].astype(F32) + self.r1[f].astype(F32)

    def s3(self):
        self.c2().wait_recv()
        self.b3[...] = (self.mine[...] + self.r2[...].astype(F32)).astype(BF)
        self.c3().start()

    def s4(self):
        self.c3().wait_recv()
        whole = self.b3[...].astype(F32) + self.r3[...].astype(F32)
        self.mine[...] = whole
        self.total[self.core] = whole[:, : self.width // 2]
        self.c4().start()

    def s5(self):
        self.c4().wait_recv()
        for c in (self.c1, self.c2, self.c3, self.c4):
            c().wait_send()


def experts_kernel(
    n_ctx, per, normed, cots, wexp, wrouter,
    x_out, gh_out, dg_out, du_out, dn_out, ff_out, gg_out,
    xs, gs, ws, gh, dg, du, own, wsem, gsem, osem, zs, zr, xsd, xr, ks, kr, *home,
):
    where = place()
    f, c, t, core, peers = where
    rows, width = normed.shape
    half = width // 2
    n_blk = 2 * n_ctx
    loads = [
        pltpu.make_async_copy(wexp.at[e, s], ws.at[s, :, pl.ds(e * 128, 128)], wsem)
        for s in range(3) for e in range(per)
    ]
    for cp in loads:
        cp.start()
    gload = pltpu.make_async_copy(cots, gs, gsem)
    gload.start()
    xs[f * n_ctx + c] = normed[...]
    greet(c, n_ctx, peers, f, t)
    ga = Gather(xs, (zs, zr, xsd, xr, ks, kr), n_ctx, where)
    ga.begin()
    n_home = len(home) // 2
    dnh = Home(home[: n_home - 2], home[n_home - 2 : n_home], where, width)
    ffh = Home(home[n_home : 2 * n_home - 2], home[2 * n_home - 2 :], where, width)
    lane = lax.broadcasted_iota(jnp.int32, (rows, 128), 1)

    def block(ff, cc, keep):
        b = ff * n_ctx + cc
        xb, gb = xs[b], gs[b, :, :width]
        lg = tdot(xb, wrouter[...], NN)
        lg = jnp.where(lane < 2 * per, lg, -1e30)
        ex = jnp.exp(lg - jnp.max(lg, -1, keepdims=True))
        gates = ex / jnp.sum(ex, -1, keepdims=True)
        gates = jnp.where(gs[b, :, width:].astype(F32) > 0.5, gates, 0.0)
        gates = jnp.where(f == 0, gates[:, :per], gates[:, per : 2 * per])
        gg = jnp.zeros((rows, 128), F32)
        for p in range(per // 2):
            cs = slice(p * 256, (p + 1) * 256)
            gv = tdot(xb, ws[0, :, cs], NN)
            uv = tdot(xb, ws[1, :, cs], NN)
            bk = tdot(gb, ws[2, :, cs], NN)
            ge = jnp.concatenate(
                [jnp.broadcast_to(gates[:, e : e + 1], (rows, 128)) for e in (2 * p, 2 * p + 1)], 1
            )
            sig = 0.5 * jnp.tanh(0.5 * gv) + 0.5
            act = gv * sig
            hid = act * uv
            dh = ge * bk
            ghv = (ge * hid).astype(BF)
            dgv = (dh * uv * (sig + act * (1.0 - sig))).astype(BF)
            duv = (dh * act).astype(BF)
            gh[b, :, cs] = ghv
            dg[b, :, cs] = dgv
            du[b, :, cs] = duv
            if keep is not None:
                own[0, keep, :, cs] = ghv
                own[1, keep, :, cs] = dgv
                own[2, keep, :, cs] = duv
                hb = hid * bk
                for i in range(2):
                    s = jnp.sum(hb[:, i * 128 : (i + 1) * 128], -1, keepdims=True)
                    gg = jnp.where(lane == f * per + 2 * p + i, s, gg)
        for i, (src, dst) in enumerate(((gh, gh_out), (dg, dg_out), (du, du_out), (xs, x_out))):
            pltpu.make_async_copy(src.at[b], dst.at[b], osem.at[i, b]).start()
        return gg

    def first(i, _):
        ff = jnp.where(i == 0, f, 1 - f)

        @pl.when(i == 1)
        def _():
            ga.cross(c)
            ga.relay(1)
            ga.ready(1 - f, c)

        gg = block(ff, c, ff)
        for h in range(2):
            dnh.part[h, ff, :, half:] = gg.astype(BF)
            ffh.part[h, ff, :, half:] = jnp.zeros((rows, 128), BF)
        return 0

    for cp in loads:
        cp.wait()
    gload.wait()
    lax.fori_loop(0, 2, first, 0)

    def dn_half(i, _):
        h = jnp.where(i == 0, 1 - core, core)
        rs = pl.ds(pl.multiple_of(h * half, 128), half)
        v = tdot(own[1].reshape(2 * rows, per * 128), ws[0, rs, :], NT)
        v = v + tdot(own[2].reshape(2 * rows, per * 128), ws[1, rs, :], NT)
        dnh.part[h, :, :, :half] = v.astype(BF).reshape(2, rows, half)
        pl.when(i == 0)(dnh.s1)
        return 0

    lax.fori_loop(0, 2, dn_half, 0)
    dnh.s2()

    def ff_half(i, _):
        h = jnp.where(i == 0, 1 - core, core)
        rs = pl.ds(pl.multiple_of(h * half, 128), half)
        v = tdot(own[0].reshape(2 * rows, per * 128), ws[2, rs, :], NT)
        ffh.part[h, :, :, :half] = v.astype(BF).reshape(2, rows, half)
        pl.when(i == 0)(ffh.s1)
        return 0

    lax.fori_loop(0, 2, ff_half, 0)
    ffh.s2()

    for j in range(1, n_ctx):
        cc = jnp.bitwise_xor(c, j)
        if j > 1:
            ga.relay(j)

        def other(i, _):
            ff = jnp.where(i == 0, f, 1 - f)
            pl.when(i == 1)(lambda: ga.cross(cc))
            ga.ready(ff, cc)
            block(ff, cc, None)
            return 0

        lax.fori_loop(0, 2, other, 0)
        if j == 1:
            dnh.s3()
        elif j == 2:
            dnh.s4()
            ffh.s3()
    ffh.s4()
    dnh.s5()
    for h in range(2):
        dn_out[:, h * half : (h + 1) * half] = dnh.total[h]
    gg_out[...] = dnh.mine[:, half:]
    ffh.s5()
    for h in range(2):
        ff_out[:, h * half : (h + 1) * half] = ffh.total[h]
    ga.finish()
    for b in range(n_blk):
        for i, (src, dst) in enumerate(((gh, gh_out), (dg, dg_out), (du, du_out), (xs, x_out))):
            pltpu.make_async_copy(src.at[b], dst.at[b], osem.at[i, b]).wait()


def experts_call(normed, cots, wexp, wrouter, n_ctx):
    rows, width = normed.shape
    per = wexp.shape[0]
    n_blk = 2 * n_ctx
    hid = per * 128
    anyspace = pl.BlockSpec(memory_space=pl.ANY)
    vmem = pl.BlockSpec(memory_space=VM)
    dma = pltpu.SemaphoreType.DMA
    home = Home.scratch(rows, width) + [dma((4,)), dma((4,))]
    shapes = [
        ((n_blk, rows, width), BF),
        ((n_blk, rows, hid), BF),
        ((n_blk, rows, hid), BF),
        ((n_blk, rows, hid), BF),
        ((rows, width), F32),
        ((rows, width), F32),
        ((rows, 128), F32),
    ]
    return pl.pallas_call(
        functools.partial(experts_kernel, n_ctx, per),
        out_shape=[jax.ShapeDtypeStruct(s, d) for s, d in shapes],
        in_specs=[vmem, anyspace, anyspace, vmem],
        out_specs=[anyspace] * 4 + [vmem] * 3,
        scratch_shapes=[
            VM((n_blk, rows, width), BF),
            VM((n_blk, rows, width + 128), BF),
            VM((3, width, hid), BF),
            VM((n_blk, rows, hid), BF),
            VM((n_blk, rows, hid), BF),
            VM((n_blk, rows, hid), BF),
            VM((3, 2, rows, hid), BF),
            dma, dma, dma((4, n_blk)),
            *Gather.sems(n_ctx),
            *home, *home,
        ],
        compiler_params=pltpu.CompilerParams(collective_id=2, has_side_effects=True, vmem_limit_bytes=62 << 20),
        name="experts",
    )(normed, cots, wexp, wrouter)


def ancestry(parents):
    blocks = parents.shape[-1]
    diagonal = jnp.eye(blocks, dtype=jnp.int32)
    upward = (parents[..., :, None] == jnp.arange(blocks, dtype=jnp.int32)).astype(jnp.int32)
    closure = jnp.minimum(diagonal + upward, 1)
    for squaring in range(blocks.bit_length()):
        closure = jnp.minimum(jnp.matmul(closure, closure), 1)
    return closure


def dot(spec, a, b):
    return jnp.einsum(spec, a, b, preferred_element_type=F32)


def swap_halves(u):
    half = u.shape[-1] // 2
    return jnp.concatenate([-u[..., half:], u[..., :half]], -1)


def norm_scale(z):
    return lax.rsqrt(jnp.mean(z * z, -1, keepdims=True) + EPS)


def norm_back(z, scale, gain, grad):
    u = grad * gain
    out = scale * u - z * (scale**3) * jnp.mean(u * z, -1, keepdims=True)
    return out, jnp.sum(grad * z * scale, 0)


def per_device(
    residual_in,
    token_mask,
    parent_blocks,
    expert_routes,
    attn_gain,
    query_weight,
    key_weight,
    value_weight,
    output_weight,
    ffn_gain,
    router_weight,
    expert_weights,
    out_cotangent,
):
    _, rows, width = residual_in.shape
    tree_len = token_mask.shape[1]
    blocks = parent_blocks.shape[1]
    experts_here = expert_weights.shape[0]
    ctx = lax.axis_index("context")
    fs = lax.axis_index("fsdp")
    n_fs = lax.axis_size("fsdp")
    n_ctx = lax.axis_size("context")
    experts = experts_here * n_fs

    stream = residual_in[0].astype(F32)
    cot = out_cotangent[0]
    routes = expert_routes[0]
    used = jnp.any(routes[:, :, None] == jnp.arange(experts, dtype=jnp.int32), 1)
    fused = n_fs == 2 and n_ctx == 4
    cot_low = cot.astype(BF)
    if fused:
        cot_low = jnp.concatenate([cot_low, jnp.pad(used.astype(BF), ((0, 0), (0, 128 - experts)))], 1)
    cot_all = lax.all_gather(cot_low, ("fsdp", "context"), axis=0, tiled=True)
    gain_one = lax.all_gather(attn_gain, "fsdp", axis=0, tiled=True).astype(F32)
    gain_two = lax.all_gather(ffn_gain, "fsdp", axis=0, tiled=True).astype(F32)
    w_qkv = jnp.concatenate([query_weight, key_weight, value_weight], 1)
    w_qkv = lax.all_gather(w_qkv, "fsdp", axis=0, tiled=True)
    w_out = lax.all_gather(output_weight, "fsdp", axis=1, tiled=True)
    w_router = lax.all_gather(router_weight, "fsdp", axis=0, tiled=True)

    heads = query_weight.shape[1] // HEAD_DIM
    kv = key_weight.shape[1] // HEAD_DIM
    group = heads // kv
    q_cols, kv_cols = heads * HEAD_DIM, kv * HEAD_DIM

    positions = ctx * rows + jnp.arange(rows, dtype=jnp.int32)
    pick = (positions[:, None] // SEG == jnp.arange(blocks, dtype=jnp.int32)[None, :]).astype(jnp.int32)
    closure = ancestry(parent_blocks[0])
    row_reach = jnp.matmul(pick, closure)
    depth = jnp.matmul(pick, jnp.sum(closure, -1) - 1)
    rope_pos = (depth * SEG + positions % SEG).astype(F32)
    half_freq = 10000.0 ** (-(jnp.arange(HEAD_DIM // 2, dtype=F32) * 2.0) / HEAD_DIM)
    angles = rope_pos[:, None, None] * jnp.concatenate([half_freq, half_freq])
    cos, sin = jnp.cos(angles), jnp.sin(angles)
    key_pos = jnp.arange(tree_len, dtype=jnp.int32)
    allowed = (
        (jnp.repeat(row_reach, SEG, axis=1) > 0)
        & (key_pos[None, :] <= positions[:, None])
        & (token_mask[0][None, :] > 0)
    )

    scale_one = norm_scale(stream)
    normed_one = (stream * scale_one * gain_one).astype(BF)
    qkv = dot("ld,dc->lc", normed_one, w_qkv)

    def rot(u):
        u = u.reshape(rows, -1, HEAD_DIM)
        return (u * cos + swap_halves(u) * sin).astype(BF).reshape(rows, -1)

    def unrot(u):
        u = u.reshape(rows, -1, HEAD_DIM)
        return (u * cos - swap_halves(u) * sin).astype(BF).reshape(rows, -1)

    q = rot(qkv[:, :q_cols]).reshape(rows, kv, group, HEAD_DIM)
    k_own = rot(qkv[:, q_cols : q_cols + kv_cols])
    v_own = qkv[:, q_cols + kv_cols :].astype(BF)
    kv_all = lax.all_gather(jnp.concatenate([k_own, v_own], 1), "context", axis=0, tiled=True)
    k_all = kv_all[:, :kv_cols].reshape(tree_len, kv, HEAD_DIM)
    v_all = kv_all[:, kv_cols:].reshape(tree_len, kv, HEAD_DIM)

    scores = dot("lkgh,mkh->kglm", q, k_all) * 0.125
    masked = jnp.where(allowed, scores, -jnp.inf)
    peak = jnp.max(masked, -1, keepdims=True)
    log_total = peak + jnp.log(jnp.sum(jnp.exp(masked - peak), -1, keepdims=True))
    probs = jnp.exp(masked - log_total)
    probs_low = probs.astype(BF)
    attended = dot("kglm,mkh->lkgh", probs_low, v_all).astype(BF).reshape(rows, q_cols)
    attn_out = lax.psum(dot("lc,cd->ld", attended, w_out).astype(BF), "tensor").astype(F32)
    middle = stream + attn_out
    scale_two = norm_scale(middle)
    normed_two = (middle * scale_two * gain_two).astype(BF)

    logits = dot("ld,de->le", normed_two, w_router)
    router_probs = jax.nn.softmax(logits, -1)
    gates = jnp.where(used, router_probs, 0.0)

    if fused:
        x_all, gated_hid, d_gate_val, d_up_val, dn, ffn_out, gate_grad = experts_call(
            normed_two, cot_all.reshape(n_fs * n_ctx, rows, -1), expert_weights,
            jnp.pad(w_router, ((0, 0), (0, 128 - experts))), n_ctx
        )
        gate_grad = gate_grad[:, :experts]
        block_out = middle + ffn_out
        normed_all = x_all.reshape(-1, width)
        gated_hid, d_gate_val, d_up_val = (
            z.reshape(-1, experts_here, 128) for z in (gated_hid, d_gate_val, d_up_val)
        )
        expert_grad = jnp.stack(
            [
                dot("td,tef->edf", normed_all, d_gate_val),
                dot("td,tef->edf", normed_all, d_up_val),
                dot("td,tef->edf", cot_all[:, :width], gated_hid),
            ],
            1,
        )
    else:
        normed_all = lax.all_gather(normed_two, ("fsdp", "context"), axis=0, tiled=True)
        gates_all = lax.all_gather(gates, ("fsdp", "context"), axis=0, tiled=True)
        gates_here = lax.dynamic_slice_in_dim(gates_all, fs * experts_here, experts_here, 1)
        g3 = gates_here[:, :, None]
        gate_val = dot("td,edf->tef", normed_all, expert_weights[:, 0])
        up_val = dot("td,edf->tef", normed_all, expert_weights[:, 1])
        back = dot("td,edf->tef", cot_all, expert_weights[:, 2])
        sig = 1.0 / (1.0 + jnp.exp(-gate_val))
        act = gate_val * sig
        hid = act * up_val
        gated_hid = (g3 * hid).astype(BF)
        gate_grad_part = jnp.sum(hid * back, -1)
        d_hid = g3 * back
        d_gate_val = (d_hid * up_val * (sig * (1.0 + gate_val * (1.0 - sig)))).astype(BF)
        d_up_val = (d_hid * act).astype(BF)

        def own(z):
            z = z.reshape((n_fs, n_ctx, rows) + z.shape[1:])
            return lax.dynamic_index_in_dim(z, ctx, 1, keepdims=False)

        ffn_part = dot("stef,edf->std", own(gated_hid), expert_weights[:, 2])
        dn_part = dot("stef,edf->std", own(d_gate_val), expert_weights[:, 0]) + dot(
            "stef,edf->std", own(d_up_val), expert_weights[:, 1]
        )
        gate_part = lax.dynamic_update_slice_in_dim(
            jnp.zeros((n_fs, rows, experts), F32), own(gate_grad_part), fs * experts_here, 2
        )

        def home(z):
            z = lax.psum_scatter(z.astype(BF), "fsdp", scatter_dimension=0, tiled=True)
            return lax.psum(z, "tensor").astype(F32)[0]

        dn = home(dn_part)
        gate_grad = lax.psum(lax.psum_scatter(gate_part, "fsdp", scatter_dimension=0, tiled=True), "tensor")[0]
        ffn_out = home(ffn_part)
        block_out = middle + ffn_out

        expert_grad = jnp.stack(
            [
                dot("td,tef->edf", normed_all, d_gate_val),
                dot("td,tef->edf", normed_all, d_up_val),
                dot("td,tef->edf", cot_all, gated_hid),
            ],
            1,
        )

    own_mask = lax.dynamic_slice_in_dim(token_mask[0], ctx * rows, rows, 0).astype(F32)
    sums = [jnp.sum(jnp.sum(z * z, -1) * own_mask) for z in (stream, attn_out, middle, ffn_out)]
    sums = lax.psum(jnp.stack(sums + [jnp.sum(own_mask)]), ("fsdp", "context"))
    rms_stats = jnp.sqrt(sums[:4] / (sums[4] * width))

    prob_grad = jnp.where(used, gate_grad, 0.0)
    logit_grad = (router_probs * (prob_grad - jnp.sum(router_probs * prob_grad, -1, keepdims=True))).astype(BF)
    dn = dn + dot("le,de->ld", logit_grad, w_router)
    router_full = dot("ld,le->de", normed_two, logit_grad)
    mid_grad, ffn_gain_full = norm_back(middle, scale_two, gain_two, dn)
    middle_grad = cot + mid_grad
    d_attn = middle_grad.astype(BF)
    out_full = dot("lc,ld->cd", attended, d_attn)
    d_att = dot("ld,cd->lc", d_attn, w_out).astype(BF).reshape(rows, kv, group, HEAD_DIM)
    d_probs = dot("lkgh,mkh->kglm", d_att, v_all)
    delta = jnp.sum(probs * d_probs, -1, keepdims=True)
    d_scores = (probs * (d_probs - delta)).astype(BF)
    dq = dot("kglm,mkh->lkgh", d_scores, k_all) * 0.125
    dk = dot("kglm,lkgh->mkh", d_scores, q) * 0.125
    dv = dot("kglm,lkgh->mkh", probs_low, d_att)
    dkv = jnp.concatenate([dk.reshape(tree_len, kv_cols), dv.reshape(tree_len, kv_cols)], 1)
    dkv = lax.psum_scatter(dkv.astype(BF), "context", scatter_dimension=0, tiled=True).astype(F32)
    d_qkv = jnp.concatenate(
        [unrot(dq.reshape(rows, q_cols)), unrot(dkv[:, :kv_cols]), dkv[:, kv_cols:].astype(BF)], 1
    )
    qkv_full = dot("ld,lc->dc", normed_one, d_qkv)
    dn_one = lax.psum(dot("lc,dc->ld", d_qkv, w_qkv).astype(BF), "tensor").astype(F32)
    str_grad, attn_gain_full = norm_back(stream, scale_one, gain_one, dn_one)
    input_grad = middle_grad + str_grad

    qkv_part = lax.psum(lax.psum_scatter(qkv_full.astype(BF), "fsdp", scatter_dimension=0, tiled=True), "context").astype(F32)
    out_part = lax.psum(lax.psum_scatter(out_full.astype(BF), "fsdp", scatter_dimension=1, tiled=True), "context").astype(F32)
    small = jnp.concatenate([router_full, attn_gain_full[:, None], ffn_gain_full[:, None]], 1)
    small = lax.psum(lax.psum_scatter(small, "fsdp", scatter_dimension=0, tiled=True), "context")
    return (
        block_out.astype(BF)[None],
        input_grad[None],
        small[:, experts],
        qkv_part[:, :q_cols],
        qkv_part[:, q_cols : q_cols + kv_cols],
        qkv_part[:, q_cols + kv_cols :],
        out_part,
        small[:, experts + 1],
        small[:, :experts],
        expert_grad,
        rms_stats,
    )


def solution(mesh):
    return jax.shard_map(
        per_device,
        mesh=mesh,
        in_specs=(
            P("fsdp", "context", None),
            P("fsdp", None),
            P("fsdp", None),
            P("fsdp", "context", None),
            P("fsdp"),
            P("fsdp", "tensor"),
            P("fsdp", "tensor"),
            P("fsdp", "tensor"),
            P("tensor", "fsdp"),
            P("fsdp"),
            P("fsdp", None),
            P("fsdp", None, None, "tensor"),
            P("fsdp", "context", None),
        ),
        out_specs=(
            P("fsdp", "context", None),
            P("fsdp", "context", None),
            P("fsdp"),
            P("fsdp", "tensor"),
            P("fsdp", "tensor"),
            P("fsdp", "tensor"),
            P("tensor", "fsdp"),
            P("fsdp"),
            P("fsdp", None),
            P("fsdp", None, None, "tensor"),
            P(),
        ),
        check_vma=False,
    )
```

```python
import functools

import jax
import jax.numpy as jnp
from jax import lax
from jax.experimental import pallas as pl
from jax.experimental.pallas import tpu as pltpu
from jax.sharding import PartitionSpec as P

HEAD_DIM = 64
SEG = 128
EPS = 1e-06
BF = jnp.bfloat16
F32 = jnp.float32


MESH = pl.DeviceIdType.MESH
VM = pltpu.VMEM
DMA = pltpu.SemaphoreType.DMA
NN, NT, TN = ((1,), (0,)), ((1,), (1,)), ((0,), (0,))


def tdot(a, b, dims):
    return lax.dot_general(a, b, (dims, ((), ())), preferred_element_type=F32)


def place():
    f, c, t = lax.axis_index("fsdp"), lax.axis_index("context"), lax.axis_index("tensor")
    core, y = lax.rem(t, 2), t // 2
    peers = dict(x=(1 - f, c, t), core=(f, c, t + 1 - 2 * core), y=(f, c, lax.rem(t + 2, 4)))
    return f, c, t, core, y, peers


def greet(where, n_ctx):
    f, c, t, core, y, peers = where
    bar = pltpu.get_barrier_semaphore()
    others = [(1 - f, c, t), peers["core"], peers["y"]]
    for k in range(1, n_ctx):
        cc = lax.rem(c + k, n_ctx)
        others += [(f, cc, t), (1 - f, cc, t)]
    for p in others:
        pl.semaphore_signal(bar, inc=1, device_id=p, device_id_type=MESH)
    pl.semaphore_wait(bar, len(others))


def remote(src, dst, send, recv, device):
    return pltpu.make_async_remote_copy(
        src_ref=src, dst_ref=dst, send_sem=send, recv_sem=recv, device_id=device, device_id_type=MESH
    )


class Spread:
    def __init__(self, buf, sems, n, where, cross_src=None):
        self.buf, self.n = buf, n
        self.f, self.c, self.t, self.core, self.y, self.peers = where
        self.rows, self.half = buf.shape[1] // 2, buf.shape[2] // 2
        self.cross_src = cross_src
        self.xs, self.xr, self.zs, self.zr, self.ys, self.yr, self.ks, self.kr = sems

    @staticmethod
    def sems(n):
        return [DMA, DMA, DMA((2, 2, n)), DMA((2, n)), DMA((2, n)), DMA((2, n)), DMA((2, 2, n)), DMA((2, 2, n))]

    def cut(self, ref, y, core):
        return ref.at[
            pl.ds(pl.multiple_of(y * self.rows, self.rows), self.rows),
            pl.ds(pl.multiple_of(core * self.half, 128), self.half),
        ]

    def part(self, f, c, y, core):
        return self.cut(self.buf.at[f * self.n + c], y, core)

    def x(self):
        dst = self.part(self.f, self.c, self.y, self.core)
        src = dst if self.cross_src is None else self.cut(self.cross_src, self.y, self.core)
        return remote(src, dst, self.xs, self.xr, self.peers["x"])

    def z(self, side, f, c):
        r = self.part(f, c, self.y, self.core)
        return remote(r, r, self.zs.at[(side + 1) // 2, f, c], self.zr.at[f, c], (self.f, self.c + side, self.t))

    def yy(self, f, c):
        r = self.part(f, c, self.y, self.core)
        return remote(r, r, self.ys.at[f, c], self.yr.at[f, c], self.peers["y"])

    def k(self, y, f, c):
        r = self.part(f, c, y, self.core)
        return remote(r, r, self.ks.at[y, f, c], self.kr.at[y, f, c], self.peers["core"])

    def there(self, c):
        return (c >= 0) & (c < self.n)

    def begin(self):
        self.x().start()
        for side in (-1, 1):
            pl.when(self.there(self.c + side))(lambda side=side: self.z(side, self.f, self.c).start())

    def first(self):
        g, c = 1 - self.f, self.c
        self.x().wait_recv()
        self.yy(g, c).start()
        for side in (-1, 1):
            pl.when(self.there(c + side))(lambda side=side: self.z(side, g, c).start())
        self.k(self.y, g, c).start()

    def relay(self, d, trees=(0, 1)):
        for tree in trees:
            f = self.f if tree == 0 else 1 - self.f
            for side in (-1, 1):
                block = self.c + side * d

                @pl.when(self.there(block))
                def _(f=f, side=side, block=block):
                    self.z(-side, f, block).wait_recv()
                    pl.when(self.there(self.c - side))(lambda: self.z(-side, f, block).start())
                    self.yy(f, block).start()
                    self.k(self.y, f, block).start()

    def over(self, f, c):
        self.yy(f, c).wait_recv()
        self.k(1 - self.y, f, c).start()

    def over_at(self, d):
        for side in (-1, 1):
            block = self.c + side * d

            @pl.when(self.there(block))
            def _(block=block):
                self.over(self.f, block)
                self.over(1 - self.f, block)

    def ready(self, f, c):
        for y in range(2):
            self.k(y, f, c).wait_recv()

    def all_ready(self):
        for g in range(2):
            for b in range(self.n):
                pl.when((g != self.f) | (b != self.c))(lambda g=g, b=b: self.ready(g, b))

    def finish(self):
        n, c = self.n, self.c
        self.x().wait_send()
        for g in range(2):
            for b in range(n):

                @pl.when((g != self.f) | (b != c))
                def _(g=g, b=b):
                    self.yy(g, b).wait_send()
                    for y in range(2):
                        self.k(y, g, b).wait_send()

                pl.when((b >= c) & (c > 0))(lambda g=g, b=b: self.z(-1, g, b).wait_send())
                pl.when((b <= c) & (c < n - 1))(lambda g=g, b=b: self.z(1, g, b).wait_send())


class Line:
    def __init__(self, buf, sems, n, where):
        self.buf, self.n = buf, n
        self.f, self.c, self.t, self.core, self.y, self.peers = where
        self.xs, self.xr, self.zs, self.zr = sems

    @staticmethod
    def sems(n):
        return [DMA((n,)), DMA((n,)), DMA((2, n)), DMA((n,))]

    def z(self, side, c):
        r = self.buf.at[self.f * self.n + c]
        return remote(r, r, self.zs.at[(side + 1) // 2, c], self.zr.at[c], (self.f, self.c + side, self.t))

    def x(self, c):
        r = self.buf.at[self.f * self.n + c]
        return remote(r, r, self.xs.at[c], self.xr.at[c], self.peers["x"])

    def there(self, c):
        return (c >= 0) & (c < self.n)

    def begin(self):
        self.x(self.c).start()
        for side in (-1, 1):
            pl.when(self.there(self.c + side))(lambda side=side: self.z(side, self.c).start())

    def relay(self, d):
        for side in (-1, 1):
            block = self.c + side * d

            @pl.when(self.there(block))
            def _(side=side, block=block):
                self.z(-side, block).wait_recv()
                pl.when(self.there(self.c - side))(lambda: self.z(-side, block).start())
                self.x(block).start()

    def crossed(self, c):
        self.x(c).wait_recv()

    def finish(self):
        n, c = self.n, self.c
        for b in range(n):
            self.x(b).wait_send()
            pl.when((b >= c) & (c > 0))(lambda b=b: self.z(-1, b).wait_send())
            pl.when((b <= c) & (c < n - 1))(lambda b=b: self.z(1, b).wait_send())


class Total:
    def __init__(self, refs, sems, where):
        self.part, self.r1, self.b3, self.r3, self.total = refs
        self.send, self.recv = sems
        self.f, self.c, self.t, self.core, self.y, self.peers = where

    @staticmethod
    def scratch(rows, width):
        w = width // 2
        return [VM((2, rows, w), BF), VM((rows, w), BF), VM((rows, w), BF), VM((rows, w), BF), VM((2, rows, w), F32), DMA((3,)), DMA((3,))]

    def copy(self, i, src, dst, to):
        return remote(src, dst, self.send.at[i], self.recv.at[i], self.peers[to])

    def c1(self):
        return self.copy(0, self.part.at[1 - self.core], self.r1, "core")

    def c3(self):
        return self.copy(1, self.b3, self.r3, "y")

    def c4(self):
        r = self.total.at[self.core]
        return self.copy(2, r, r, "core")

    def s1(self):
        self.c1().start()

    def s2(self):
        self.c1().wait_recv()
        self.b3[...] = (self.part[self.core].astype(F32) + self.r1[...].astype(F32)).astype(BF)
        self.c3().start()

    def s3(self):
        self.c3().wait_recv()
        self.total[self.core] = self.b3[...].astype(F32) + self.r3[...].astype(F32)
        self.c4().start()

    def s4(self):
        self.c4().wait_recv()
        for c in (self.c1, self.c3, self.c4):
            c().wait_send()


def front_kernel(
    n, heads, kvs, experts, bits, resid, cot, routes, tokens, cos, sin, pack, wq, wk, wv, wo,
    gs_out, n1_out, ut_out, n2_out, mid_out, rp_out, att_out, q_out, kv_out, lse_out, mask_out, used_out, wqkv, wout, wrt, gains,
    gs, n1s, ut, packs, n1, wosem, wsend, wrecv, usend, urecv, ksend, krecv, osem, *rest,
):
    where = place()
    f, c, t, core, y, peers = where
    rows, width = resid.shape
    half = width // 2
    qc, kc = heads * HEAD_DIM, kvs * HEAD_DIM
    group = heads // kvs
    me = f * n + c
    g = 1 - f
    lane = lax.broadcasted_iota(jnp.int32, (rows, 128), 1)
    used = jnp.zeros((rows, 128), F32)
    for j in range(routes.shape[1]):
        used = jnp.where(routes[:, j : j + 1] == lane, 1.0, used)
    used_out[...] = used
    gs[me] = cot[...].astype(BF)
    ut[me] = used.T[:experts].astype(BF)
    packs[f] = pack[...]
    local = [
        pltpu.make_async_copy(src, wqkv.at[f, :, pl.ds(at, src.shape[1])], wosem.at[i])
        for i, (src, at) in enumerate(((wq, 0), (wk, qc), (wv, qc + kc)))
    ] + [pltpu.make_async_copy(wo, wout.at[f], wosem.at[3])]
    for cp in local:
        cp.start()
    greet(where, n)
    cross = [remote(pack, packs.at[f], wsend.at[0], wrecv.at[0], peers["x"])]
    for i, (src, at) in enumerate(((wq, 0), (wk, qc), (wv, qc + kc))):
        cross.append(remote(src, wqkv.at[f, :, pl.ds(at, src.shape[1])], wsend.at[1 + i], wrecv.at[1 + i], peers["x"]))
    cross.append(remote(wo, wout.at[f], wsend.at[4], wrecv.at[4], peers["x"]))
    for cp in cross[:4]:
        cp.start()
    gn = Spread(gs, rest[:8], n, where)
    gn.begin()
    cross[4].start()

    def used_pushes():
        for k in range(n):
            for i, ff in enumerate((f, g)):
                if k or i:
                    cc = lax.rem(c + k, n)
                    yield remote(ut.at[me], ut.at[me], usend.at[i, k], urecv.at[me], (ff, cc, t))

    for cp in used_pushes():
        cp.start()

    total = n * rows
    row = lax.broadcasted_iota(jnp.int32, (rows, total), 0)
    col = lax.broadcasted_iota(jnp.int32, (rows, total), 1)
    block = lax.broadcasted_iota(jnp.int32, (1, total), 1) // SEG
    reach = [jnp.bitwise_and(lax.shift_right_logical(jnp.full((1, total), bits[i], jnp.int32), block), 1) for i in range(2)]
    seen = jnp.where(row < SEG, reach[0], reach[1]) * tokens[...]
    seen = (seen > 0) & (col <= row + c * rows)
    mask_out[...] = jnp.where(seen, 1.0, 0.0).astype(BF)

    stream = resid[...].astype(F32)
    cross[0].wait_recv()
    for h in range(2):
        gains[:, h * half : (h + 1) * half] = packs[h, 16:32, :].astype(F32)[:8]
        wrt[:, h * half : (h + 1) * half] = jnp.zeros((128, half), BF)
        wrt[0:16, h * half : (h + 1) * half] = packs[h, 0:16, :]
    scale = lax.rsqrt(jnp.mean(stream * stream, -1, keepdims=True) + EPS)
    n1[...] = (stream * scale * gains[0:1, :]).astype(BF)
    fcols = pl.ds(pl.multiple_of(f * half, 128), half)
    gcols = pl.ds(pl.multiple_of(g * half, 128), half)
    n1s[me] = n1[:, fcols]
    for cp in local[:3]:
        cp.wait()
    acc = tdot(n1[:, fcols], wqkv[f], NN)
    gn.relay(1, (0,))
    for cp in cross[1:4]:
        cp.wait_recv()
    acc = acc + tdot(n1[:, gcols], wqkv[g], NN)

    def turn(u):
        cols = u.shape[1]
        return (u * widen(cos[...], cols) + swap32(u) * widen(sin[...], cols)).astype(BF)

    q_out[...] = turn(acc[:, :qc])
    mine = pl.ds(pl.multiple_of(c * rows, rows), rows)
    kv_out[mine, :kc] = turn(acc[:, qc : qc + kc])
    kv_out[mine, kc:] = acc[:, qc + kc :].astype(BF)

    def kv_push(k):
        r = kv_out.at[mine]
        return remote(r, r, ksend.at[k - 1], krecv.at[k - 1], (f, lax.rem(c + k, n), t))

    for k in range(1, n):
        kv_push(k).start()
    nn = Spread(n1s, rest[8:16], n, where, n1.at[:, gcols])
    tot = Total(rest[16:21], rest[21:23], where)
    gn.first()
    gn.relay(2, (0,))
    nn.begin()
    for k in range(1, n):
        kv_push(k).wait_recv()

    lse_out[...] = jnp.zeros((rows, 128), F32)
    seen = mask_out[...].astype(F32) > 0.5
    steps = [
        lambda: gn.over(g, c),
        lambda: gn.relay(1, (1,)),
        lambda: gn.relay(3, (0,)),
        lambda: (gn.over_at(1), nn.first()),
        lambda: (gn.relay(2, (1,)), nn.relay(1, (0,))),
        lambda: (gn.over_at(2), nn.over(g, c)),
    ]
    for h in range(heads):
        j = h // group
        hs = slice(h * HEAD_DIM, (h + 1) * HEAD_DIM)
        kj, vj = kv_out[:, j * HEAD_DIM : (j + 1) * HEAD_DIM], kv_out[:, kc + j * HEAD_DIM : kc + (j + 1) * HEAD_DIM]
        s = jnp.where(seen, tdot(q_out[:, hs], kj, NT) * 0.125, -1e30)
        peak = jnp.max(s, -1, keepdims=True)
        e = jnp.exp(s - peak)
        z = jnp.sum(e, -1, keepdims=True)
        p = (e * (1.0 / z)).astype(BF)
        att_out[:, hs] = tdot(p, vj, NN).astype(BF)
        lse_out[:, h : h + 1] = peak + jnp.log(z)
        if h < len(steps):
            steps[h]()
    local[3].wait()
    cross[4].wait_recv()

    def project(i, _):
        h = jnp.where(i == 0, 1 - core, core)
        tot.part[h] = tdot(att_out[...], wout[h], NN).astype(BF)
        pl.when(i == 0)(tot.s1)
        return 0

    lax.fori_loop(0, 2, project, 0)
    tot.s2()
    gn.relay(3, (1,))
    nn.relay(1, (1,))
    nn.relay(2, (0,))
    gn.over_at(3)
    nn.over_at(1)
    tot.s3()
    nn.relay(2, (1,))
    nn.relay(3, (0,))
    tot.s4()
    middle = stream + jnp.concatenate([tot.total[0], tot.total[1]], 1)
    mid_out[...] = middle
    scale = lax.rsqrt(jnp.mean(middle * middle, -1, keepdims=True) + EPS)
    n2 = (middle * scale * gains[1:2, :]).astype(BF)
    n2_out[...] = n2
    logits = jnp.where(lane < experts, tdot(n2, wrt[...], NT), -1e30)
    e = jnp.exp(logits - jnp.max(logits, -1, keepdims=True))
    rp_out[...] = e / jnp.sum(e, -1, keepdims=True)
    nn.over_at(2)
    nn.relay(3, (1,))
    nn.over_at(3)
    gn.all_ready()
    nn.all_ready()
    outs = [pltpu.make_async_copy(gs, gs_out, osem.at[0]), pltpu.make_async_copy(n1s, n1_out, osem.at[1])]
    for cp in outs:
        cp.start()
    for b in range(2 * n):

        @pl.when(b != me)
        def _(b=b):
            remote(ut.at[b], ut.at[b], usend.at[0, 0], urecv.at[b], peers["x"]).wait_recv()

    ut_out[...] = ut[...]
    for cp in used_pushes():
        cp.wait_send()
    for cp in cross:
        cp.wait_send()
    for k in range(1, n):
        kv_push(k).wait_send()
    gn.finish()
    nn.finish()
    for cp in outs:
        cp.wait()


def front_call(n, heads, kvs, experts, bits, vmem_ins, hbm_ins):
    resid = vmem_ins[0]
    rows, width = resid.shape
    half = width // 2
    qc, kc = heads * HEAD_DIM, kvs * HEAD_DIM
    hbm = pl.BlockSpec(memory_space=pl.ANY)
    vmem = pl.BlockSpec(memory_space=VM)
    shapes = [
        ((2 * n, rows, width), BF),
        ((2 * n, rows, half), BF),
        ((2 * n, experts, rows), BF),
        ((rows, width), BF),
        ((rows, width), F32),
        ((rows, 128), F32),
        ((rows, qc), BF),
        ((rows, qc), BF),
        ((n * rows, 2 * kc), BF),
        ((rows, 128), F32),
        ((rows, n * rows), BF),
        ((rows, 128), F32),
        ((2, half, qc + 2 * kc), BF),
        ((2, qc, half), BF),
        ((128, width), BF),
        ((8, width), F32),
    ]
    return pl.pallas_call(
        functools.partial(front_kernel, n, heads, kvs, experts),
        out_shape=[jax.ShapeDtypeStruct(s, d) for s, d in shapes],
        in_specs=[pl.BlockSpec(memory_space=pltpu.SMEM)] + [vmem] * len(vmem_ins) + [hbm] * len(hbm_ins),
        out_specs=[hbm] * 2 + [vmem] * 14,
        scratch_shapes=[
            VM((2 * n, rows, width), BF),
            VM((2 * n, rows, half), BF),
            VM((2 * n, experts, rows), BF),
            VM((2, 32, half), BF),
            VM((rows, width), BF),
            DMA((4,)), DMA((5,)), DMA((5,)), DMA((2, n)), DMA((2 * n,)), DMA((n - 1,)), DMA((n - 1,)), DMA((2,)),
            *Spread.sems(n),
            *Spread.sems(n),
            *Total.scratch(rows, width),
        ],
        compiler_params=pltpu.CompilerParams(collective_id=1, has_side_effects=True, vmem_limit_bytes=63 << 20),
        name="front",
    )(bits, *vmem_ins, *hbm_ins)


class Home:
    def __init__(self, refs, sems, where, width):
        self.part, self.r1, self.mine, self.b2, self.r2, self.b3, self.r3, self.total = refs
        self.send, self.recv = sems
        self.f, self.c, self.t, self.core, self.y, self.peers = where
        self.width = width

    @staticmethod
    def scratch(rows, width):
        w = width // 2 + 128
        return [
            VM((2, 2, rows, w), BF),
            VM((2, rows, w), BF),
            VM((rows, w), F32),
            VM((rows, w), BF),
            VM((rows, w), BF),
            VM((rows, w), BF),
            VM((rows, w), BF),
            VM((2, rows, width // 2), F32),
            DMA((4,)),
            DMA((4,)),
        ]

    def copy(self, i, src, dst, to):
        return remote(src, dst, self.send.at[i], self.recv.at[i], self.peers[to])

    def c1(self):
        return self.copy(0, self.part.at[1 - self.core], self.r1, "core")

    def c2(self):
        return self.copy(1, self.b2, self.r2, "x")

    def c3(self):
        return self.copy(2, self.b3, self.r3, "y")

    def c4(self):
        r = self.total.at[self.core]
        return self.copy(3, r, r, "core")

    def s1(self):
        self.c1().start()

    def s2(self):
        self.c1().wait_recv()
        f, core = self.f, self.core
        self.b2[...] = (self.part[core, 1 - f].astype(F32) + self.r1[1 - f].astype(F32)).astype(BF)
        self.c2().start()
        self.mine[...] = self.part[core, f].astype(F32) + self.r1[f].astype(F32)

    def s3(self):
        self.c2().wait_recv()
        self.b3[...] = (self.mine[...] + self.r2[...].astype(F32)).astype(BF)
        self.c3().start()

    def s4(self):
        self.c3().wait_recv()
        whole = self.b3[...].astype(F32) + self.r3[...].astype(F32)
        self.mine[...] = whole
        self.total[self.core] = whole[:, : self.width // 2]
        self.c4().start()

    def s5(self):
        self.c4().wait_recv()
        for c in (self.c1, self.c2, self.c3, self.c4):
            c().wait_send()


def masked_squares(z, rowmask):
    z = jnp.sum(z * z * rowmask, 0, keepdims=True)
    return sum(z[:, i * 128 : (i + 1) * 128] for i in range(z.shape[1] // 128))


def experts_kernel(
    n, per, normed, cots, wexp, wrt, used_t, attended, middle, resid, rowmask,
    att_out, x_out, gh_out, dg_out, du_out, dn_out, bo_out, gg_out, sq_out,
    xs, gs, ws, stage, own, atts, wsem, gsem, osem, asem, *rest,
):
    where = place()
    f, c, t, core, y, peers = where
    rows, width = normed.shape
    half = width // 2
    loads = [
        pltpu.make_async_copy(wexp.at[e, s], ws.at[s, :, pl.ds(e * 128, 128)], wsem)
        for s in range(3) for e in range(per)
    ]
    for cp in loads:
        cp.start()
    gload = pltpu.make_async_copy(cots, gs, gsem)
    gload.start()
    xs[f * n + c] = normed[...]
    greet(where, n)
    ga = Spread(xs, rest[:8], n, where)
    ga.begin()
    dnh = Home(rest[8:16], rest[16:18], where, width)
    ffh = Home(rest[18:26], rest[26:28], where, width)
    an = Line(atts, rest[28:32], n, where)
    atts[f * n + c] = attended[...]
    lane = lax.broadcasted_iota(jnp.int32, (rows, 128), 1)
    outs = (gh_out, dg_out, du_out)

    def sends(b, src):
        copies = [pltpu.make_async_copy(src.at[i], out.at[b], osem.at[i, b]) for i, out in enumerate(outs)]
        return copies + [pltpu.make_async_copy(xs.at[b], x_out.at[b], osem.at[3, b])]

    def block(ff, cc, dst, keep):
        b = ff * n + cc
        xb, gb = xs[b], gs[b]
        lg = tdot(xb, wrt[...], NT)
        lg = jnp.where(lane < 2 * per, lg, -1e30)
        ex = jnp.exp(lg - jnp.max(lg, -1, keepdims=True))
        gates = ex / jnp.sum(ex, -1, keepdims=True)
        used = jnp.concatenate([used_t[b].astype(F32), jnp.zeros((128 - 2 * per, rows), F32)], 0).T
        gates = jnp.where(used > 0.5, gates, 0.0)
        gates = jnp.where(f == 0, gates[:, :per], gates[:, per : 2 * per])
        gg = jnp.zeros((rows, 128), F32)
        for p in range(per // 2):
            cs = slice(p * 256, (p + 1) * 256)
            gv = tdot(xb, ws[0, :, cs], NN)
            uv = tdot(xb, ws[1, :, cs], NN)
            bk = tdot(gb, ws[2, :, cs], NN)
            ge = jnp.concatenate(
                [jnp.broadcast_to(gates[:, e : e + 1], (rows, 128)) for e in (2 * p, 2 * p + 1)], 1
            )
            sig = 0.5 * jnp.tanh(0.5 * gv) + 0.5
            act = gv * sig
            hid = act * uv
            dh = ge * bk
            ghv = (ge * hid).astype(BF)
            dgv = (dh * uv * (sig + act * (1.0 - sig))).astype(BF)
            duv = (dh * act).astype(BF)
            dst[0, :, cs] = ghv
            dst[1, :, cs] = dgv
            dst[2, :, cs] = duv
            if keep:
                hb = hid * bk
                for i in range(2):
                    s = jnp.sum(hb[:, i * 128 : (i + 1) * 128], -1, keepdims=True)
                    gg = jnp.where(lane == f * per + 2 * p + i, s, gg)
        for cp in sends(b, dst):
            cp.start()
        return gg

    def first(i, _):
        ff = jnp.where(i == 0, f, 1 - f)

        @pl.when(i == 1)
        def _():
            ga.first()
            ga.over(1 - f, c)
            ga.relay(1)
            ga.ready(1 - f, c)

        gg = block(ff, c, own.at[:, ff], True)
        for h in range(2):
            dnh.part[h, ff, :, half:] = gg.astype(BF)
            ffh.part[h, ff, :, half:] = jnp.zeros((rows, 128), BF)
        return 0

    for cp in loads:
        cp.wait()
    gload.wait()
    lax.fori_loop(0, 2, first, 0)

    def dn_half(i, _):
        h = jnp.where(i == 0, 1 - core, core)
        rs = pl.ds(pl.multiple_of(h * half, 128), half)
        v = tdot(own[1].reshape(2 * rows, per * 128), ws[0, rs, :], NT)
        v = v + tdot(own[2].reshape(2 * rows, per * 128), ws[1, rs, :], NT)
        dnh.part[h, :, :, :half] = v.astype(BF).reshape(2, rows, half)
        pl.when(i == 0)(dnh.s1)
        return 0

    lax.fori_loop(0, 2, dn_half, 0)
    dnh.s2()

    def ff_half(i, _):
        h = jnp.where(i == 0, 1 - core, core)
        rs = pl.ds(pl.multiple_of(h * half, 128), half)
        v = tdot(own[0].reshape(2 * rows, per * 128), ws[2, rs, :], NT)
        ffh.part[h, :, :, :half] = v.astype(BF).reshape(2, rows, half)
        pl.when(i == 0)(ffh.s1)
        return 0

    lax.fori_loop(0, 2, ff_half, 0)
    ffh.s2()
    an.begin()

    for j in range(1, n):
        cc = jnp.bitwise_xor(c, j)
        if j > 1:
            ga.relay(j)
        ga.over(f, cc)

        def other(i, _):
            ff = jnp.where(i == 0, f, 1 - f)
            ga.ready(ff, cc)
            pl.when(i == 0)(lambda: ga.over(1 - f, cc))
            if j > 1:
                for cp in sends(ff * n + jnp.bitwise_xor(c, j - 1), stage.at[i])[:3]:
                    cp.wait()
            block(ff, cc, stage.at[i], False)
            return 0

        lax.fori_loop(0, 2, other, 0)
        an.relay(j)
        if j == 1:
            dnh.s3()
        elif j == 2:
            dnh.s4()
            ffh.s3()
    ffh.s4()
    dnh.s5()
    for h in range(2):
        dn_out[:, h * half : (h + 1) * half] = dnh.total[h]
    gg_out[...] = dnh.mine[:, half:]
    mid, stream, mask = middle[...], resid[...].astype(F32), rowmask[:, :1]
    sq_out[...] = jnp.zeros((8, 128), F32)
    for i, z in enumerate((stream, mid - stream, mid)):
        sq_out[i : i + 1, :] = masked_squares(z, mask)
    sq_out[4:5, :] = jnp.sum(rowmask[...], 0, keepdims=True)
    ffh.s5()
    squares = jnp.zeros((1, 128), F32)
    for h in range(2):
        cs = slice(h * half, (h + 1) * half)
        bo_out[:, cs] = (middle[:, cs] + ffh.total[h]).astype(BF)
        squares = squares + masked_squares(ffh.total[h], mask)
    sq_out[3:4, :] = squares
    for b in range(n):
        an.crossed(b)
    acopy = pltpu.make_async_copy(atts, att_out, asem)
    acopy.start()
    ga.finish()
    an.finish()
    acopy.wait()
    for ff in (f, 1 - f):
        for j in range(n):
            waits = sends(ff * n + jnp.bitwise_xor(c, j), stage.at[0])
            for cp in waits if j in (0, n - 1) else waits[3:]:
                cp.wait()


def experts_call(normed, cots, wexp, wrt, used_t, attended, middle, resid, rowmask, n):
    rows, width = normed.shape
    per = wexp.shape[0]
    hid = per * 128
    hbm = pl.BlockSpec(memory_space=pl.ANY)
    vmem = pl.BlockSpec(memory_space=VM)
    shapes = [
        ((2 * n,) + attended.shape, BF),
        ((2 * n, rows, width), BF),
        ((2 * n, rows, hid), BF),
        ((2 * n, rows, hid), BF),
        ((2 * n, rows, hid), BF),
        ((rows, width), F32),
        ((rows, width), BF),
        ((rows, 128), F32),
        ((8, 128), F32),
    ]
    return pl.pallas_call(
        functools.partial(experts_kernel, n, per),
        out_shape=[jax.ShapeDtypeStruct(s, d) for s, d in shapes],
        in_specs=[vmem, hbm, hbm] + [vmem] * 6,
        out_specs=[hbm] * 5 + [vmem] * 4,
        scratch_shapes=[
            VM((2 * n, rows, width), BF),
            VM((2 * n, rows, width), BF),
            VM((3, width, hid), BF),
            VM((2, 3, rows, hid), BF),
            VM((3, 2, rows, hid), BF),
            VM((2 * n,) + attended.shape, BF),
            DMA, DMA, DMA((4, 2 * n)), DMA,
            *Spread.sems(n),
            *Home.scratch(rows, width),
            *Home.scratch(rows, width),
            *Line.sems(n),
        ],
        compiler_params=pltpu.CompilerParams(collective_id=2, has_side_effects=True, vmem_limit_bytes=63 << 20),
        name="experts",
    )(normed, cots, wexp, wrt, used_t, attended, middle, resid, rowmask)


def swap32(u):
    lanes = lax.broadcasted_iota(jnp.int32, u.shape, 1)
    size = u.shape[1]
    return jnp.where(lax.rem(lanes, 64) < 32, pltpu.roll(u, size - 32, 1), pltpu.roll(u, 32, 1))


def widen(table, cols):
    return jnp.concatenate([table] * (cols // 128), 1) if cols > 128 else table


def turn_back(u, cos, sin):
    cols = u.shape[1]
    return u * widen(cos, cols) - swap32(u) * widen(sin, cols)


def rms_back(z, gain, grad):
    scale = lax.rsqrt(jnp.mean(z * z, -1, keepdims=True) + EPS)
    u = grad * gain
    out = scale * u - z * (scale * scale * scale) * jnp.mean(u * z, -1, keepdims=True)
    return out, jnp.sum(grad * z * scale, 0, keepdims=True)


def backward_kernel(
    n, heads, kvs, dn, gg, rp, used, wrt, middle, cot, resid, gains, wout, wqkv, q, kv, lse, mask, cos, sin, sq,
    x_all, cots, gh, dg, du, att_all, n1_all,
    ig_out, qkv_out, wo_out, router_out, small_out, we_out,
    xg, pin, pout, atts, n1, das, dqs, dks, dmid, dlow, dkv, push, got, smallb, smalls,
    lsem, pisem, posem, psend, precv, tsend, trecv, *rest,
):
    where = place()
    f, c, t, core, y, peers = where
    rows, width = middle.shape
    half = width // 2
    qc, kc = heads * HEAD_DIM, kvs * HEAD_DIM
    group = heads // kvs
    me = f * n + c
    loads = []
    for b in range(2 * n):
        rs = pl.ds(b * rows, rows)
        loads.append(pltpu.make_async_copy(x_all.at[b], xg.at[0, rs], lsem.at[0]))
        loads.append(pltpu.make_async_copy(cots.at[b], xg.at[1, rs], lsem.at[0]))
        loads.append(pltpu.make_async_copy(att_all.at[b], atts.at[rs], lsem.at[0]))
        loads.append(pltpu.make_async_copy(n1_all.at[b], n1.at[rs], lsem.at[0]))
    n_pair = gh.shape[2] // 256
    n_work = 3 * n_pair

    def pin_copies(i, slot, src):
        cols = pl.ds(pl.multiple_of(lax.rem(i, n_pair) * 256, 256), 256)
        return [
            pltpu.make_async_copy(src.at[b, :, cols], pin.at[slot, pl.ds(b * rows, rows)], pisem.at[slot]) for b in range(2 * n)
        ]

    def pin_start(i):
        slot = lax.rem(i, 2)
        for s, src in enumerate((dg, du, gh)):

            @pl.when((i >= s * n_pair) & (i < (s + 1) * n_pair))
            def _(src=src):
                for cp in pin_copies(i, slot, src):
                    cp.start()

    def pout_copies(i):
        slot = lax.rem(i, 2)
        e = 2 * lax.rem(i, n_pair)
        return [
            pltpu.make_async_copy(pout.at[slot, :, pl.ds(k * 128, 128)], we_out.at[e + k, i // n_pair], posem.at[slot, k])
            for k in range(2)
        ]

    def work(i, _):
        slot = lax.rem(i, 2)
        for cp in pin_copies(i, slot, dg):
            cp.wait()
        v = tdot(xg[i // (2 * n_pair)], pin[slot], TN)

        @pl.when(i >= 2)
        def _():
            for cp in pout_copies(i - 2):
                cp.wait()

        pout[slot] = v.astype(BF)
        for cp in pout_copies(i):
            cp.start()
        pl.when(i + 2 < n_work)(lambda: pin_start(i + 2))
        return 0

    for cp in loads:
        cp.start()
    for i in range(2):
        pin_start(jnp.int32(i))
    greet(where, n)

    p = rp[...]
    pg = jnp.where(used[...] > 0.5, gg[...], 0.0)
    dl = (p * (pg - jnp.sum(p * pg, -1, keepdims=True))).astype(BF)
    dnt = dn[...] + tdot(dl, wrt[...], NN)
    mg, g2 = rms_back(middle[...], gains[1:2, :], dnt)
    mg = cot[...] + mg
    dmid[...] = mg
    low = mg.astype(BF)
    dlow[...] = low
    dan = Spread(das, rest[:8], n, where, dlow.at[:, pl.ds(pl.multiple_of((1 - f) * half, 128), half)])
    das[me] = dlow[:, pl.ds(pl.multiple_of(f * half, 128), half)]
    dan.begin()
    dqn = Line(dqs, rest[8:12], n, where)
    dkn = Line(dks, rest[12:16], n, where)
    tot = Total(rest[16:21], rest[21:23], where)
    dqs[me, :, qc:] = dl

    d_att = (tdot(low[:, :half], wout[0], NT) + tdot(low[:, half:], wout[1], NT)).astype(BF)
    seen = mask[...].astype(F32) > 0.5
    dq = []
    for j in range(kvs):
        kj, vj = kv[:, j * HEAD_DIM : (j + 1) * HEAD_DIM], kv[:, kc + j * HEAD_DIM : kc + (j + 1) * HEAD_DIM]
        dkj = dvj = None
        for g in range(group):
            h = j * group + g
            hs = slice(h * HEAD_DIM, (h + 1) * HEAD_DIM)
            qh, dah = q[:, hs], d_att[:, hs]
            s = jnp.where(seen, tdot(qh, kj, NT) * 0.125, -1e30)
            pr = jnp.exp(s - lse[:, h : h + 1])
            dp = tdot(dah, vj, NT)
            ds = (pr * (dp - jnp.sum(pr * dp, -1, keepdims=True))).astype(BF)
            dq.append(tdot(ds, kj, NN) * 0.125)
            dkh = tdot(ds, qh, TN)
            dvh = tdot(pr.astype(BF), dah, TN)
            dkj = dkh if g == 0 else dkj + dkh
            dvj = dvh if g == 0 else dvj + dvh
        dkv[:, j * HEAD_DIM : (j + 1) * HEAD_DIM] = dkj * 0.125
        dkv[:, kc + j * HEAD_DIM : kc + (j + 1) * HEAD_DIM] = dvj
        if j == 0:
            dan.first()
            dan.over(1 - f, c)
    push[...] = dkv[...].astype(BF).reshape(push.shape)

    def pushes(k):
        cc = lax.rem(c + k, n)
        return remote(push.at[cc], got.at[k - 1], psend.at[k - 1], precv.at[k - 1], (f, cc, t))

    for k in range(1, n):
        pushes(k).start()
    dqv = turn_back(jnp.concatenate(dq, 1), cos[...], sin[...]).astype(BF)
    dqs[me, :, :qc] = dqv
    dqn.begin()
    dan.relay(1)
    for cp in loads:
        cp.wait()
    lax.fori_loop(0, 3, work, 0)
    dqn.relay(1)
    own = dkv[pl.ds(pl.multiple_of(c * rows, rows), rows), :]
    for k in range(1, n):
        pushes(k).wait_recv()
        own = own + got[k - 1].astype(F32)
    dkk = turn_back(own[:, :kc], cos[...], sin[...]).astype(BF)
    dvv = own[:, kc:].astype(BF)
    dks[me, :, :kc] = dkk
    dks[me, :, kc:] = dvv
    dkn.begin()

    def n1_half(i, _):
        h = jnp.where(i == 0, 1 - core, core)
        v = tdot(dqs[me, :, :qc], wqkv[h, :, :qc], NT) + tdot(dks[me], wqkv[h, :, qc:], NT)
        tot.part[h] = v.astype(BF)
        pl.when(i == 0)(tot.s1)
        return 0

    lax.fori_loop(0, 2, n1_half, 0)
    lax.fori_loop(3, 4, work, 0)
    tot.s2()
    dqn.relay(2)
    dan.relay(2)
    lax.fori_loop(4, 6, work, 0)
    dkn.relay(1)
    dqn.relay(3)
    lax.fori_loop(6, 8, work, 0)
    tot.s3()
    dkn.relay(2)
    dan.relay(3)
    lax.fori_loop(8, 9, work, 0)
    tot.s4()
    dkn.relay(3)
    stream = resid[...].astype(F32)
    dn1 = jnp.concatenate([tot.total[0], tot.total[1]], 1)
    sg, g1 = rms_back(stream, gains[0:1, :], dn1)
    ig_out[...] = dmid[...] + sg
    for h in range(2):
        hs = slice(h * half, (h + 1) * half)
        smallb[h] = jnp.zeros(smallb.shape[1:], F32)
        smallb[h, 0:1, :half] = g2[:, hs]
        smallb[h, 1:2, :half] = g1[:, hs]
        smallb[h, :, half:] = sq[...]
    smalls[me] = smallb[f]

    def tails():
        for k in range(1, n):
            cc = lax.rem(c + k, n)
            for i, ff in enumerate((f, 1 - f)):
                yield remote(smallb.at[ff], smalls.at[me], tsend.at[i, k], trecv.at[me], (ff, cc, t))
        yield remote(smallb.at[1 - f], smalls.at[me], tsend.at[1, 0], trecv.at[me], (1 - f, c, t))

    for cp in tails():
        cp.start()
    for j in range(1, n):
        cc = jnp.bitwise_xor(c, j)
        dan.over(f, cc)
        dan.over(1 - f, cc)
    lax.fori_loop(9, n_work, work, 0)
    dan.ready(1 - f, c)
    for j in range(1, n):
        cc = jnp.bitwise_xor(c, j)
        dan.ready(f, cc)
        dan.ready(1 - f, cc)
    wo_out[...] = tdot(atts[...], das[...].reshape(2 * n * rows, half), TN)
    for b in range(n):
        dqn.crossed(b)
    qkv_out[:, :qc] = tdot(n1[...], dqs[:, :, :qc].reshape(2 * n * rows, qc), TN)
    router_out[...] = tdot(
        xg[0, :, pl.ds(pl.multiple_of(f * half, 128), half)], dqs[:, :, qc:].reshape(2 * n * rows, 128), TN
    )
    for b in range(n):
        dkn.crossed(b)
    qkv_out[:, qc:] = tdot(n1[...], dks[...].reshape(2 * n * rows, 2 * kc), TN)
    for b in range(2 * n):

        @pl.when(b != me)
        def _(b=b):
            remote(smallb.at[0], smalls.at[b], tsend.at[0, 0], trecv.at[b], peers["x"]).wait_recv()

    small_out[...] = sum(smalls[b] for b in range(2 * n))
    for cp in tails():
        cp.wait_send()
    for k in range(1, n):
        pushes(k).wait_send()
    dan.finish()
    dqn.finish()
    dkn.finish()
    for i in (n_work - 2, n_work - 1):
        for cp in pout_copies(jnp.int32(i)):
            cp.wait()


def backward_call(n, heads, kvs, ins, hbm_ins):
    middle = ins[5]
    rows, width = middle.shape
    half = width // 2
    qc, kc = heads * HEAD_DIM, kvs * HEAD_DIM
    tokens = 2 * n * rows
    hid = hbm_ins[2].shape[2]
    hbm = pl.BlockSpec(memory_space=pl.ANY)
    vmem = pl.BlockSpec(memory_space=VM)
    shapes = [
        ((rows, width), F32),
        ((half, qc + 2 * kc), F32),
        ((qc, half), F32),
        ((half, 128), F32),
        ((8, half + 128), F32),
        ((hid // 128, 3, width, 128), BF),
    ]
    return pl.pallas_call(
        functools.partial(backward_kernel, n, heads, kvs),
        out_shape=[jax.ShapeDtypeStruct(s, d) for s, d in shapes],
        in_specs=[vmem] * len(ins) + [hbm] * len(hbm_ins),
        out_specs=[vmem] * 5 + [hbm],
        scratch_shapes=[
            VM((2, tokens, width), BF),
            VM((2, tokens, 256), BF),
            VM((2, width, 256), BF),
            VM((tokens, qc), BF),
            VM((tokens, half), BF),
            VM((2 * n, rows, half), BF),
            VM((2 * n, rows, qc + 128), BF),
            VM((2 * n, rows, 2 * kc), BF),
            VM((rows, width), F32),
            VM((rows, width), BF),
            VM((n * rows, 2 * kc), F32),
            VM((n, rows, 2 * kc), BF),
            VM((n - 1, rows, 2 * kc), BF),
            VM((2, 8, half + 128), F32),
            VM((2 * n, 8, half + 128), F32),
            DMA((1,)), DMA((2,)), DMA((2, 2)), DMA((n - 1,)), DMA((n - 1,)), DMA((2, n)), DMA((2 * n,)),
            *Spread.sems(n),
            *Line.sems(n),
            *Line.sems(n),
            *Total.scratch(rows, width),
        ],
        compiler_params=pltpu.CompilerParams(collective_id=3, has_side_effects=True, vmem_limit_bytes=63 << 20),
        name="backward",
    )(*ins, *hbm_ins)


def ancestry(parents):
    blocks = parents.shape[-1]
    diagonal = jnp.eye(blocks, dtype=jnp.int32)
    upward = (parents[..., :, None] == jnp.arange(blocks, dtype=jnp.int32)).astype(jnp.int32)
    closure = jnp.minimum(diagonal + upward, 1)
    for squaring in range(blocks.bit_length()):
        closure = jnp.minimum(jnp.matmul(closure, closure), 1)
    return closure


def dot(spec, a, b):
    return jnp.einsum(spec, a, b, preferred_element_type=F32)


def swap_halves(u):
    half = u.shape[-1] // 2
    return jnp.concatenate([-u[..., half:], u[..., :half]], -1)


def norm_scale(z):
    return lax.rsqrt(jnp.mean(z * z, -1, keepdims=True) + EPS)


def norm_back(z, scale, gain, grad):
    u = grad * gain
    out = scale * u - z * (scale**3) * jnp.mean(u * z, -1, keepdims=True)
    return out, jnp.sum(grad * z * scale, 0)


def per_device(
    residual_in,
    token_mask,
    parent_blocks,
    expert_routes,
    attn_gain,
    query_weight,
    key_weight,
    value_weight,
    output_weight,
    ffn_gain,
    router_weight,
    expert_weights,
    out_cotangent,
):
    _, rows, width = residual_in.shape
    tree_len = token_mask.shape[1]
    blocks = parent_blocks.shape[1]
    experts_here = expert_weights.shape[0]
    ctx = lax.axis_index("context")
    fs = lax.axis_index("fsdp")
    n_fs = lax.axis_size("fsdp")
    n_ctx = lax.axis_size("context")
    experts = experts_here * n_fs

    stream = residual_in[0].astype(F32)
    cot = out_cotangent[0]
    cot_all = lax.all_gather(cot.astype(BF), ("fsdp", "context"), axis=0, tiled=True)
    gain_one = lax.all_gather(attn_gain, "fsdp", axis=0, tiled=True).astype(F32)
    gain_two = lax.all_gather(ffn_gain, "fsdp", axis=0, tiled=True).astype(F32)
    w_qkv = jnp.concatenate([query_weight, key_weight, value_weight], 1)
    w_qkv = lax.all_gather(w_qkv, "fsdp", axis=0, tiled=True)
    w_out = lax.all_gather(output_weight, "fsdp", axis=1, tiled=True)
    w_router = lax.all_gather(router_weight, "fsdp", axis=0, tiled=True)

    heads = query_weight.shape[1] // HEAD_DIM
    kv = key_weight.shape[1] // HEAD_DIM
    group = heads // kv
    q_cols, kv_cols = heads * HEAD_DIM, kv * HEAD_DIM

    positions = ctx * rows + jnp.arange(rows, dtype=jnp.int32)
    pick = (positions[:, None] // SEG == jnp.arange(blocks, dtype=jnp.int32)[None, :]).astype(jnp.int32)
    closure = ancestry(parent_blocks[0])
    row_reach = jnp.matmul(pick, closure)
    depth = jnp.matmul(pick, jnp.sum(closure, -1) - 1)
    rope_pos = (depth * SEG + positions % SEG).astype(F32)
    half_freq = 10000.0 ** (-(jnp.arange(HEAD_DIM // 2, dtype=F32) * 2.0) / HEAD_DIM)
    angles = rope_pos[:, None, None] * jnp.concatenate([half_freq, half_freq])
    cos, sin = jnp.cos(angles), jnp.sin(angles)
    key_pos = jnp.arange(tree_len, dtype=jnp.int32)
    allowed = (
        (jnp.repeat(row_reach, SEG, axis=1) > 0)
        & (key_pos[None, :] <= positions[:, None])
        & (token_mask[0][None, :] > 0)
    )

    scale_one = norm_scale(stream)
    normed_one = (stream * scale_one * gain_one).astype(BF)
    qkv = dot("ld,dc->lc", normed_one, w_qkv)

    def rot(u):
        u = u.reshape(rows, -1, HEAD_DIM)
        return (u * cos + swap_halves(u) * sin).astype(BF).reshape(rows, -1)

    def unrot(u):
        u = u.reshape(rows, -1, HEAD_DIM)
        return (u * cos - swap_halves(u) * sin).astype(BF).reshape(rows, -1)

    q = rot(qkv[:, :q_cols]).reshape(rows, kv, group, HEAD_DIM)
    k_own = rot(qkv[:, q_cols : q_cols + kv_cols])
    v_own = qkv[:, q_cols + kv_cols :].astype(BF)
    kv_all = lax.all_gather(jnp.concatenate([k_own, v_own], 1), "context", axis=0, tiled=True)
    k_all = kv_all[:, :kv_cols].reshape(tree_len, kv, HEAD_DIM)
    v_all = kv_all[:, kv_cols:].reshape(tree_len, kv, HEAD_DIM)

    scores = dot("lkgh,mkh->kglm", q, k_all) * 0.125
    masked = jnp.where(allowed, scores, -jnp.inf)
    peak = jnp.max(masked, -1, keepdims=True)
    log_total = peak + jnp.log(jnp.sum(jnp.exp(masked - peak), -1, keepdims=True))
    probs = jnp.exp(masked - log_total)
    probs_low = probs.astype(BF)
    attended = dot("kglm,mkh->lkgh", probs_low, v_all).astype(BF).reshape(rows, q_cols)
    attn_out = lax.psum(dot("lc,cd->ld", attended, w_out).astype(BF), "tensor").astype(F32)
    middle = stream + attn_out
    scale_two = norm_scale(middle)
    normed_two = (middle * scale_two * gain_two).astype(BF)

    logits = dot("ld,de->le", normed_two, w_router)
    router_probs = jax.nn.softmax(logits, -1)
    routes = expert_routes[0]
    used = jnp.any(routes[:, :, None] == jnp.arange(experts, dtype=jnp.int32), 1)
    gates = jnp.where(used, router_probs, 0.0)

    normed_all = lax.all_gather(normed_two, ("fsdp", "context"), axis=0, tiled=True)
    gates_all = lax.all_gather(gates, ("fsdp", "context"), axis=0, tiled=True)
    gates_here = lax.dynamic_slice_in_dim(gates_all, fs * experts_here, experts_here, 1)
    g3 = gates_here[:, :, None]
    gate_val = dot("td,edf->tef", normed_all, expert_weights[:, 0])
    up_val = dot("td,edf->tef", normed_all, expert_weights[:, 1])
    back = dot("td,edf->tef", cot_all, expert_weights[:, 2])
    sig = 1.0 / (1.0 + jnp.exp(-gate_val))
    act = gate_val * sig
    hid = act * up_val
    gated_hid = (g3 * hid).astype(BF)
    gate_grad_part = jnp.sum(hid * back, -1)
    d_hid = g3 * back
    d_gate_val = (d_hid * up_val * (sig * (1.0 + gate_val * (1.0 - sig)))).astype(BF)
    d_up_val = (d_hid * act).astype(BF)

    def own(z):
        z = z.reshape((n_fs, n_ctx, rows) + z.shape[1:])
        return lax.dynamic_index_in_dim(z, ctx, 1, keepdims=False)

    ffn_part = dot("stef,edf->std", own(gated_hid), expert_weights[:, 2])
    dn_part = dot("stef,edf->std", own(d_gate_val), expert_weights[:, 0]) + dot(
        "stef,edf->std", own(d_up_val), expert_weights[:, 1]
    )
    gate_part = lax.dynamic_update_slice_in_dim(
        jnp.zeros((n_fs, rows, experts), F32), own(gate_grad_part), fs * experts_here, 2
    )

    def home(z):
        z = lax.psum_scatter(z.astype(BF), "fsdp", scatter_dimension=0, tiled=True)
        return lax.psum(z, "tensor").astype(F32)[0]

    dn = home(dn_part)
    gate_grad = lax.psum(lax.psum_scatter(gate_part, "fsdp", scatter_dimension=0, tiled=True), "tensor")[0]
    ffn_out = home(ffn_part)
    block_out = middle + ffn_out

    expert_grad = jnp.stack(
        [
            dot("td,tef->edf", normed_all, d_gate_val),
            dot("td,tef->edf", normed_all, d_up_val),
            dot("td,tef->edf", cot_all, gated_hid),
        ],
        1,
    )

    own_mask = lax.dynamic_slice_in_dim(token_mask[0], ctx * rows, rows, 0).astype(F32)
    sums = [jnp.sum(jnp.sum(z * z, -1) * own_mask) for z in (stream, attn_out, middle, ffn_out)]
    sums = lax.psum(jnp.stack(sums + [jnp.sum(own_mask)]), ("fsdp", "context"))
    rms_stats = jnp.sqrt(sums[:4] / (sums[4] * width))

    prob_grad = jnp.where(used, gate_grad, 0.0)
    logit_grad = (router_probs * (prob_grad - jnp.sum(router_probs * prob_grad, -1, keepdims=True))).astype(BF)
    dn = dn + dot("le,de->ld", logit_grad, w_router)
    router_full = dot("ld,le->de", normed_two, logit_grad)
    mid_grad, ffn_gain_full = norm_back(middle, scale_two, gain_two, dn)
    middle_grad = cot + mid_grad
    d_attn = middle_grad.astype(BF)
    out_full = dot("lc,ld->cd", attended, d_attn)
    d_att = dot("ld,cd->lc", d_attn, w_out).astype(BF).reshape(rows, kv, group, HEAD_DIM)
    d_probs = dot("lkgh,mkh->kglm", d_att, v_all)
    delta = jnp.sum(probs * d_probs, -1, keepdims=True)
    d_scores = (probs * (d_probs - delta)).astype(BF)
    dq = dot("kglm,mkh->lkgh", d_scores, k_all) * 0.125
    dk = dot("kglm,lkgh->mkh", d_scores, q) * 0.125
    dv = dot("kglm,lkgh->mkh", probs_low, d_att)
    dkv = jnp.concatenate([dk.reshape(tree_len, kv_cols), dv.reshape(tree_len, kv_cols)], 1)
    dkv = lax.psum_scatter(dkv.astype(BF), "context", scatter_dimension=0, tiled=True).astype(F32)
    d_qkv = jnp.concatenate(
        [unrot(dq.reshape(rows, q_cols)), unrot(dkv[:, :kv_cols]), dkv[:, kv_cols:].astype(BF)], 1
    )
    qkv_full = dot("ld,lc->dc", normed_one, d_qkv)
    dn_one = lax.psum(dot("lc,dc->ld", d_qkv, w_qkv).astype(BF), "tensor").astype(F32)
    str_grad, attn_gain_full = norm_back(stream, scale_one, gain_one, dn_one)
    input_grad = middle_grad + str_grad

    qkv_part = lax.psum(lax.psum_scatter(qkv_full.astype(BF), "fsdp", scatter_dimension=0, tiled=True), "context").astype(F32)
    out_part = lax.psum(lax.psum_scatter(out_full.astype(BF), "fsdp", scatter_dimension=1, tiled=True), "context").astype(F32)
    small = jnp.concatenate([router_full, attn_gain_full[:, None], ffn_gain_full[:, None]], 1)
    small = lax.psum(lax.psum_scatter(small, "fsdp", scatter_dimension=0, tiled=True), "context")
    return (
        block_out.astype(BF)[None],
        input_grad[None],
        small[:, experts],
        qkv_part[:, :q_cols],
        qkv_part[:, q_cols : q_cols + kv_cols],
        qkv_part[:, q_cols + kv_cols :],
        out_part,
        small[:, experts + 1],
        small[:, :experts],
        expert_grad,
        rms_stats,
    )


def fused_device(
    residual_in,
    token_mask,
    parent_blocks,
    expert_routes,
    attn_gain,
    query_weight,
    key_weight,
    value_weight,
    output_weight,
    ffn_gain,
    router_weight,
    expert_weights,
    out_cotangent,
):
    _, rows, width = residual_in.shape
    blocks = parent_blocks.shape[1]
    half = width // 2
    ctx, n = lax.axis_index("context"), lax.axis_size("context")
    experts = router_weight.shape[1]
    q_cols, kv_cols = query_weight.shape[1], key_weight.shape[1]
    heads, kvs = q_cols // HEAD_DIM, kv_cols // HEAD_DIM
    resid, cot = residual_in[0], out_cotangent[0]

    parents = [parent_blocks[0, b] for b in range(blocks)]
    line, depth = [jnp.int32(1)], [jnp.int32(0)]
    for b in range(1, blocks):
        line.append((1 << b) + sum(jnp.where(parents[b] == p, line[p], 0) for p in range(b)))
        depth.append(1 + sum(jnp.where(parents[b] == p, depth[p], 0) for p in range(b)))
    here = rows // SEG
    bits, depth = (lax.dynamic_slice_in_dim(jnp.stack(z), ctx * here, here) for z in (line, depth))
    index = jnp.arange(rows, dtype=jnp.int32)
    rope_pos = (jnp.where(index < SEG, depth[0], depth[1]) * SEG + index % SEG).astype(F32)
    half_freq = 10000.0 ** (-(jnp.arange(HEAD_DIM // 2, dtype=F32) * 2.0) / HEAD_DIM)
    angles = rope_pos[:, None] * jnp.tile(half_freq, 4)[None, :]
    sign = jnp.where(jnp.arange(2 * HEAD_DIM) % HEAD_DIM < HEAD_DIM // 2, -1.0, 1.0)
    cos, sin = jnp.cos(angles), jnp.sin(angles) * sign
    pack = jnp.concatenate(
        [router_weight.T, jnp.stack([attn_gain, ffn_gain]), jnp.zeros((14, half), BF)], 0
    )
    gs, n1_all, used_t, n2, middle, rp, attended, q, kv, lse, mask, used, wqkv, wout, wrt, gains = front_call(
        n, heads, kvs, experts, bits, (resid, cot, expert_routes[0], token_mask, cos, sin, pack),
        (query_weight, key_weight, value_weight, output_weight),
    )
    row_mask = lax.dynamic_slice_in_dim(token_mask[0], ctx * rows, rows, 0).astype(F32)
    att_all, x_all, gh, dg, du, dn, block_out, gate_grad, squares = experts_call(
        n2, gs, expert_weights, wrt, used_t, attended, middle, resid, jnp.broadcast_to(row_mask[:, None], (rows, 128)), n
    )
    ins = (
        dn, gate_grad, rp, used, wrt, middle, cot, resid, gains, wout, wqkv, q, kv, lse, mask, cos, sin, squares,
    )
    input_grad, qkv_grad, out_grad, router_grad, small, expert_grad = backward_call(
        n, heads, kvs, ins, (x_all, gs, gh, dg, du, att_all, n1_all)
    )
    sums = jnp.sum(small[:5, half:], 1)
    return (
        block_out[None],
        input_grad[None],
        small[1, :half],
        qkv_grad[:, :q_cols],
        qkv_grad[:, q_cols : q_cols + kv_cols],
        qkv_grad[:, q_cols + kv_cols :],
        out_grad,
        small[0, :half],
        router_grad[:, :experts],
        expert_grad.astype(F32),
        jnp.sqrt(sums[:4] / (sums[4] / 128.0 * width)),
    )


def solution(mesh):
    small = mesh.shape["fsdp"] == 2 and mesh.shape["context"] == 4 and mesh.shape["tensor"] == 4
    return jax.shard_map(
        fused_device if small else per_device,
        mesh=mesh,
        in_specs=(
            P("fsdp", "context", None),
            P("fsdp", None),
            P("fsdp", None),
            P("fsdp", "context", None),
            P("fsdp"),
            P("fsdp", "tensor"),
            P("fsdp", "tensor"),
            P("fsdp", "tensor"),
            P("tensor", "fsdp"),
            P("fsdp"),
            P("fsdp", None),
            P("fsdp", None, None, "tensor"),
            P("fsdp", "context", None),
        ),
        out_specs=(
            P("fsdp", "context", None),
            P("fsdp", "context", None),
            P("fsdp"),
            P("fsdp", "tensor"),
            P("fsdp", "tensor"),
            P("fsdp", "tensor"),
            P("tensor", "fsdp"),
            P("fsdp"),
            P("fsdp", None),
            P("fsdp", None, None, "tensor"),
            P(),
        ),
        check_vma=False,
    )
```
